32 devices in a mesh: parts: 2 (over x), scene: 4 (over y, core), range: 4 (over z).
Axes of the slice: x: 2, y: 2, z: 4, core: 2. Of those that a mesh axis runs over, the one named last changes fastest.
Arguments:
- secondary: bfloat16 [16, 1056, 2, 1024], P(('parts', 'scene'), None, None, 'range'), parts along dimension 0, may hold values from -6 to 6
- reference_store: bfloat16 [8, 4, 256, 2, 1024], P(('parts', 'scene'), None, None, None, 'range'), parts along dimension 0, may hold values from -6 to 6
- tile_owner: int32 [8], P('parts'), parts along dimension 0, may hold values from 0 to 3
- az_kernel: float32 [64, 8], replicated, may hold values from -2 to 2
- rg_kernel: float32 [64, 8], replicated, may hold values from -2 to 2
- az_offset: int32 [16, 1024], P(('parts', 'scene')), parts along dimension 0, may hold values from -12 to 12
- az_index: int32 [16, 1024], P(('parts', 'scene')), parts along dimension 0, may hold values from 0 to 63
- rg_offset: int32 [16, 1024], P(('parts', 'scene'), 'range'), parts along dimension 0, may hold values from -12 to 12
- rg_index: int32 [16, 1024], P(('parts', 'scene'), 'range'), parts along dimension 0, may hold values from 0 to 63
Outputs:
- reference_pairs: float32 [16, 2, 256, 64], P(('parts', 'scene'), None, None, 'range'), parts along dimension 0
- sequential_pairs: float32 [16, 2, 256, 64], P(('parts', 'scene'), None, None, 'range'), parts along dimension 0
- coherence: float32 [16, 256, 64], P(('parts', 'scene'), None, 'range'), parts along dimension 0
The draws below stay inside these ranges and needn't reach their ends.
There are 2 independent parts, one for each index of `parts`. The reference program is written for one: setup_inputs(seed, part) draws one part's arguments, and reference() takes and returns one part's arrays. A program takes and returns all parts, laid end to end along the dimension named above; an argument that names none is the same for every part. Nothing has to cross between parts.
Inputs may be any that keep to these rules, and one draw needn't show every extreme that they name: `tile_owner`: the scene device holding reference tile s.
All inputs are finite; a program needn't handle non-finite values.
Results may differ from the reference program's by a relative error of at most 0.008.
Values may be sent and summed in bfloat16 or wider, within the bound.
A program may use at most 128 MiB of HBM per device.

```python
from functools import partial
import jax
import jax.numpy as jnp
from jax import lax

CDEV = 256
TILE = 256
NSTEP = 4
TAPS = 8
NKER = 64
MAXOFF = 12
LOOK_AZ = 4
LOOK_RG = 16
PAD = 16
SCENES = 8
RANGE = 1024
ROWS = 1024
N_SCENE = 4
N_RANGE = 4


def set_ends(result, key, low, top_value):
    place = [jax.random.randint(jax.random.fold_in(key, axis), (), 0, length) for axis, length in enumerate(result.shape)]
    longest = result.shape.index(max(result.shape))
    next_to = place[:longest] + [(place[longest] + 1) % result.shape[longest]] + place[longest + 1:]
    return result.at[tuple(place)].set(low).at[tuple(next_to)].set(top_value)


def block_scale(own_key, shape, shards, smallest, largest):
    loudness, own = 1.0, jax.random.fold_in(own_key, 6)
    for position, parts in shards:
        draws = jnp.exp(jax.random.uniform(jax.random.fold_in(own, position), (parts,), jnp.float32, smallest / len(shards), largest / len(shards)))
        loudness = loudness * jnp.repeat(draws, shape[position] // parts).reshape([-1 if axis == position else 1 for axis in range(len(shape))])
    return loudness


def normal_values(own_key, shape, spread, reach, cuts=(), kind=jnp.bfloat16):
    loudness = block_scale(own_key, shape, cuts, -0.22, 0.18) if cuts else 1.0
    array = jax.random.normal(own_key, shape, jnp.float32) * spread * loudness
    return jnp.minimum(jnp.maximum(array, -reach), reach).astype(kind)


def setup_inputs(seed: int = 0, part: int = 0) -> dict:
    streams_of = jax.random.split(jax.random.key(seed), 10)
    part_keys = jax.random.split(jax.random.fold_in(streams_of[9], part), 10)
    return {
        "secondary": normal_values(part_keys[0], (SCENES, ROWS + 2 * PAD, 2, RANGE), 1.0, 6.0, ((0, 4), (3, 4))),
        "reference_store": normal_values(part_keys[1], (N_SCENE, NSTEP, TILE, 2, RANGE), 1.0, 6.0, ((0, 4), (4, 4))),
        "tile_owner": set_ends(jax.random.randint(part_keys[2], (NSTEP,), 0, N_SCENE), jax.random.fold_in(part_keys[2], 1), 0, N_SCENE - 1).astype(jnp.int32),
        "az_kernel": normal_values(streams_of[3], (NKER, TAPS), 0.35, 2.0, (), jnp.float32),
        "rg_kernel": normal_values(streams_of[4], (NKER, TAPS), 0.35, 2.0, (), jnp.float32),
        "az_offset": set_ends(jax.random.randint(part_keys[5], (SCENES, ROWS), 0 - MAXOFF, MAXOFF + 1), jax.random.fold_in(part_keys[5], 1), 0 - MAXOFF, MAXOFF).astype(jnp.int32),
        "az_index": set_ends(jax.random.randint(part_keys[6], (SCENES, ROWS), 0, NKER), jax.random.fold_in(part_keys[6], 1), 0, NKER - 1).astype(jnp.int32),
        "rg_offset": set_ends(jax.random.randint(part_keys[7], (SCENES, RANGE), 0 - MAXOFF, MAXOFF + 1), jax.random.fold_in(part_keys[7], 1), 0 - MAXOFF, MAXOFF).astype(jnp.int32),
        "rg_index": set_ends(jax.random.randint(part_keys[8], (SCENES, RANGE), 0, NKER), jax.random.fold_in(part_keys[8], 1), 0, NKER - 1).astype(jnp.int32),
    }


eps_power = 1e-06

def band_matrix(tap_values, offsets, margin):
    length = offsets.shape[0]
    row_base = jnp.arange(length, dtype=jnp.int32) + offsets + (margin - 3)
    columns = jnp.arange(length + 2 * margin, dtype=jnp.int32)
    matrix = jnp.zeros((length, length + 2 * margin), jnp.float32)
    for tap_index in range(tap_values.shape[1]):
        matrix = matrix + jnp.where(columns[None, :] == (row_base + tap_index)[:, None], tap_values[:, tap_index:tap_index + 1], 0.0)
    return matrix.astype(jnp.bfloat16)

def multilook(sample):
    scenes, height, breadth = sample.shape
    blocks = sample.reshape(scenes, height // LOOK_AZ, LOOK_AZ, breadth // LOOK_RG, LOOK_RG)
    return lax.optimization_barrier(jnp.mean(blocks, axis=(2, 4)))

def products(reference_tile, current, earlier):
    cur_val = current.astype(jnp.float32)
    cur_re, cur_im = (cur_val[:, :, 0], cur_val[:, :, 1])
    pri_val = earlier.astype(jnp.float32)
    pri_re, pri_im = (pri_val[:, :, 0], pri_val[:, :, 1])
    ref_val = reference_tile.astype(jnp.float32)[None]
    ref_re, ref_im = (ref_val[:, :, 0], ref_val[:, :, 1])
    pair_re = multilook(ref_re * cur_re + ref_im * cur_im)
    pair_im = multilook(ref_im * cur_re - ref_re * cur_im)
    seq_re = multilook(pri_re * cur_re + pri_im * cur_im)
    seq_im = multilook(pri_im * cur_re - pri_re * cur_im)
    power_earlier = multilook(pri_re * pri_re + pri_im * pri_im)
    power_current = multilook(cur_re * cur_re + cur_im * cur_im)
    magnitude = jnp.sqrt(seq_re * seq_re + seq_im * seq_im)
    coherent = magnitude / jnp.sqrt(power_earlier * power_current + eps_power)
    return (jnp.stack([pair_re, pair_im], 1), jnp.stack([seq_re, seq_im], 1), coherent)

def reference(secondary, reference_store, tile_owner, az_kernel, rg_kernel, az_offset, az_index, rg_offset, rg_index):
    banded = jax.vmap(partial(band_matrix, margin=PAD))
    widened = jnp.pad(secondary, ((0, 0), (0, 0), (0, 0), (PAD, PAD)))
    rg_taps = rg_kernel[rg_index]
    pair_parts, seq_parts, coh_parts = ([], [], [])
    for tile_step in range(NSTEP):
        row_start = tile_step * TILE
        reference_tile = lax.dynamic_index_in_dim(reference_store, tile_owner[tile_step], 0, keepdims=False)[tile_step]
        tile_rows = widened[:, row_start:row_start + TILE + 2 * PAD]
        az_taps = az_kernel[az_index[:, row_start:row_start + TILE]]
        az_matrix = banded(az_taps, az_offset[:, row_start:row_start + TILE])
        az_result = jnp.einsum('skq,sqpw->skpw', az_matrix.astype(jnp.float32), tile_rows.astype(jnp.float32)).astype(jnp.bfloat16)
        pieces = []
        for column_block in range(N_RANGE):
            col_start = column_block * CDEV
            rg_matrix = banded(rg_taps[:, col_start:col_start + CDEV], rg_offset[:, col_start:col_start + CDEV])
            window = az_result[..., col_start:col_start + CDEV + 2 * PAD].astype(jnp.float32)
            pieces.append(jnp.einsum('skpw,scw->skpc', window, rg_matrix.astype(jnp.float32)).astype(jnp.bfloat16))
        current = jnp.concatenate(pieces, -1)
        earlier = jnp.concatenate([reference_tile[None], current[:-1]], 0)
        pair_out, seq_out, coh_out = products(reference_tile, current, earlier)
        pair_parts.append(pair_out)
        seq_parts.append(seq_out)
        coh_parts.append(coh_out)
    return (jnp.concatenate(pair_parts, 2), jnp.concatenate(seq_parts, 2), jnp.concatenate(coh_parts, 1))
```

```python
import functools

import jax
import jax.numpy as jnp
from jax import lax
from jax.experimental import pallas as pl
from jax.experimental.pallas import tpu as pltpu
from jax.sharding import PartitionSpec as P

LOOK_AZ = 4
LOOK_RG = 16
LANES = 128

eps_power = 1e-06
F32 = jnp.float32
BF16 = jnp.bfloat16
MESH = pl.DeviceIdType.MESH


def iota(shape, dim):
    return lax.broadcasted_iota(jnp.int32, shape, dim)


def flag(condition):
    return jnp.where(condition, 1.0, 0.0).astype(BF16)


def matmul(a, b, contract=((1,), (0,))):
    return lax.dot_general(a, b, (contract, ((), ())), preferred_element_type=F32)


def tap_table(kernel, stride):
    count, taps = kernel.shape
    place = flag(iota((taps, LANES), 1) == stride * iota((taps, LANES), 0))
    spread = matmul(kernel.astype(BF16), place).astype(BF16)
    ones = flag(iota((16, LANES), 0) == 0)
    return jnp.concatenate(
        [
            jnp.concatenate([spread, jnp.zeros((count, LANES), BF16)], 1),
            jnp.concatenate([jnp.zeros((16, LANES), BF16), ones], 1),
        ],
        0,
    )


def looked_up(table, index, offset):
    count = table.shape[0] - 16
    length = index.shape[1]
    one_hot = flag(iota((count, length), 0) == index)
    shift = jnp.broadcast_to(offset.astype(F32), (16, length)).astype(BF16)
    return matmul(jnp.concatenate([one_hot, shift], 0), table, ((0,), (0,)))


def banded(taps, place, reach):
    inside = (place >= 0) & (place < reach)
    picked = jnp.take_along_axis(taps, place & (LANES - 1), axis=1, mode="promise_in_bounds")
    return jnp.where(inside, picked, 0.0).astype(BF16)


def kernel_body(
    dims,
    sec_hbm, store_hbm, owner_ref, azk_ref, rgk_ref, azo_ref, azi_ref, rgo_ref, rgi_ref,
    pair_ref, seq_ref, coh_ref,
    sec, store, own, z, cur, az_mat, rg_mat, rg_halo, table, perm, edge, halo,
    recv_f, recv_b, send_f, send_b, ret_s, ret_r,
    sec_sem, store_sem, edge_sem, halo_sem, fs_sem, fr_sem, bs_sem, br_sem, rs_sem, rr_sem,
):
    scenes, tiles, rows, cols, margin, taps, n_scene, n_range = dims
    looks = rows // LOOK_AZ
    cells = cols // LOOK_RG
    wide = 2 * (rows + 2 * margin)
    both = 2 * rows
    me = lax.axis_index("scene")
    col = lax.axis_index("range")
    at_first, at_last = me == 0, me == n_scene - 1
    has_left, has_right = col > 0, col < n_range - 1
    sides = (
        (has_left, {"range": col - 1}),
        (has_right, {"range": col + 1}),
        (me > 0, {"scene": me - 1}),
        (me < n_scene - 1, {"scene": me + 1}),
    )

    def load_store(s):
        source = store_hbm.reshape(tiles, both, cols).at[s]
        return pltpu.make_async_copy(source, store.at[s], store_sem.at[s])

    def load_sec(k):
        length = sec.shape[1]
        source = sec_hbm.reshape(scenes, length, cols).at[k]
        return pltpu.make_async_copy(source, sec.at[k], sec_sem.at[k])

    for k in range(scenes):
        load_sec(k).start()
    for s in range(tiles):
        load_store(s).start()

    barrier = pltpu.get_barrier_semaphore()
    for exists, device in sides:
        @pl.when(exists)
        def _():
            pl.semaphore_signal(barrier, inc=1, device_id=device, device_id_type=MESH)

    @pl.when(jnp.logical_not(has_left))
    def _():
        halo[:, 0] = jnp.zeros(halo.shape[:1] + halo.shape[2:], BF16)

    @pl.when(jnp.logical_not(has_right))
    def _():
        halo[:, 1] = jnp.zeros(halo.shape[:1] + halo.shape[2:], BF16)

    @pl.when(at_first)
    def _():
        recv_f[...] = jnp.zeros_like(recv_f)
        ret_r[...] = jnp.zeros_like(ret_r)

    @pl.when(at_last)
    def _():
        recv_b[...] = jnp.zeros_like(recv_b)

    table[...] = tap_table(azk_ref[...], 2)
    order = iota((rows, rows), 0)
    perm[...] = flag(iota((rows, rows), 1) == LOOK_AZ * (order % looks) + order // looks)
    rg_table = tap_table(rgk_ref[...], 1)
    for k in range(scenes):
        found = looked_up(rg_table, rgi_ref[k : k + 1, :], rgo_ref[k : k + 1, :])
        tap_rows, shift = found[:, :LANES], found[:, LANES:].astype(jnp.int32)
        lane = iota((cols, LANES), 1)
        start = iota((cols, LANES), 0) + shift + (margin - 3)
        for t in range(cols // LANES):
            rg_mat[k, :, t * LANES : (t + 1) * LANES] = banded(
                tap_rows, lane + (t * LANES + margin) - start, taps
            )
        beside = jnp.where(lane < margin, lane, lane + cols)
        beside = jnp.where(lane < 2 * margin, beside, 4 * cols)
        outer = banded(tap_rows, beside - start, taps).astype(F32)
        rg_halo[k] = jnp.transpose(outer)[: 2 * margin].astype(BF16)

    def edge_copy(s, side):
        to = {"range": col - 1} if side == 0 else {"range": col + 1}
        return pltpu.make_async_remote_copy(
            src_ref=edge.at[s, side],
            dst_ref=halo.at[s, 1 - side],
            send_sem=edge_sem.at[s, side],
            recv_sem=halo_sem.at[s, 1 - side],
            device_id=to,
            device_id_type=MESH,
        )

    def halo_arrival(s, side):
        return edge_copy(s, 1 - side)

    def line_copy(s, forward):
        if forward:
            source, target, sent, got, to = send_f, recv_f, fs_sem, fr_sem, me + 1
        else:
            source, target, sent, got, to = send_b, recv_b, bs_sem, br_sem, me - 1
        return pltpu.make_async_remote_copy(
            src_ref=source.at[s],
            dst_ref=target.at[s],
            send_sem=sent.at[s],
            recv_sem=got.at[s],
            device_id={"scene": to},
            device_id_type=MESH,
        )

    def result_copy(s):
        return pltpu.make_async_remote_copy(
            src_ref=ret_s.at[s],
            dst_ref=ret_r.at[s],
            send_sem=rs_sem.at[s],
            recv_sem=rr_sem.at[s],
            device_id={"scene": me + 1},
            device_id_type=MESH,
        )

    def azimuth(s):
        for k in range(scenes):
            here = pl.ds(pl.multiple_of(s * rows, rows), rows)
            found = looked_up(table[...], azi_ref[k : k + 1, here], azo_ref[k : k + 1, here])
            found = matmul(perm[...], found.astype(BF16))
            for l in range(LOOK_AZ):
                part = found[l * looks : (l + 1) * looks]
                tap_rows, shift = part[:, :LANES], part[:, LANES:].astype(jnp.int32)
                row = LOOK_AZ * iota((looks, LANES), 0) + l
                start = iota((looks, LANES), 1) - 2 * (row + shift + (margin - 3))
                for p in range(2):
                    for t in range(az_mat.shape[1] // LANES):
                        top = p * rows + l * looks
                        az_mat[top : top + looks, t * LANES : (t + 1) * LANES] = banded(
                            tap_rows, start + (t * LANES - p), 2 * taps
                        )
            lines = sec[k, pl.ds(pl.multiple_of(s * both, both), wide), :]
            z[s, k] = matmul(az_mat[:, :wide], lines).astype(BF16)
            which = iota((2 * margin, cols), 0)
            which = jnp.where(which < margin, which, which + cols - 2 * margin)
            ends = matmul(flag(iota((2 * margin, cols), 1) == which), z[s, k], ((1,), (1,)))
            ends = ends.astype(BF16)
            edge[s, 0, k] = ends[:margin]
            edge[s, 1, k] = ends[margin:]

        @pl.when(has_left)
        def _():
            edge_copy(s, 0).start()

        @pl.when(has_right)
        def _():
            edge_copy(s, 1).start()

    def range_step(s):
        @pl.when(has_left)
        def _():
            halo_arrival(s, 0).wait_recv()

        @pl.when(has_right)
        def _():
            halo_arrival(s, 1).wait_recv()

        for k in range(scenes):
            beside = jnp.concatenate([halo[s, 0, k], halo[s, 1, k]], 0)
            total = matmul(z[s, k], rg_mat[k], ((1,), (1,)))
            total = total + matmul(beside, rg_halo[k], ((0,), (0,)))
            cur[s, k] = total.astype(BF16)

    def pass_on(s, forward, from_here):
        owner = owner_ref[s]
        if forward:
            instead = cur[s, scenes - 1]
            if not from_here:
                line_copy(s, True).wait_recv()
                instead = jnp.where(owner < me, recv_f[s], instead)
            send_f[s] = jnp.where(owner == me, own[s], instead)
        else:
            instead = cur[s, 0]
            if not from_here:
                line_copy(s, False).wait_recv()
                instead = jnp.where(owner > me, recv_b[s], instead)
            send_b[s] = jnp.where(owner == me, own[s], instead)
        line_copy(s, forward).start()

    inner = jnp.logical_not(at_first) & jnp.logical_not(at_last)
    early_f = inner & (me == 1)
    early_b = inner & (me == n_scene - 2) & jnp.logical_not(early_f)

    def early(s):
        @pl.when(early_f)
        def _():
            pass_on(s, True, False)

        @pl.when(early_b)
        def _():
            pass_on(s, False, False)

    for k in range(scenes):
        load_sec(k).wait()
    pl.semaphore_wait(barrier, sum(exists.astype(jnp.int32) for exists, _ in sides))
    azimuth(0)
    for s in range(tiles):
        load_store(s).wait()
    line = iota((both, both), 0)
    pick = 2 * (LOOK_AZ * (line % looks) + (line % rows) // looks) + line // rows
    pick = flag(iota((both, both), 1) == pick)
    for s in range(tiles):
        own[s] = matmul(pick, store[s]).astype(BF16)

    def resample(s, carry):
        @pl.when(s + 1 < tiles)
        def _():
            azimuth(s + 1)

        range_step(s)

        @pl.when(at_first)
        def _():
            pass_on(s, True, True)

        @pl.when(at_last)
        def _():
            pass_on(s, False, True)

        @pl.when(s > 0)
        def _():
            early(s - 1)

        return carry

    lax.fori_loop(0, tiles, resample, 0)
    early(tiles - 1)

    mean = flag(iota((cols, cells), 0) // LOOK_RG == iota((cols, cells), 1))

    def row_sums(*makers):
        sums = None
        for l in range(LOOK_AZ):
            terms = makers[0](l)
            sums = terms if sums is None else [a + b for a, b in zip(sums, terms)]
        return sums

    def multilooked(sums):
        stacked = jnp.concatenate(sums, 0)
        high = stacked.astype(BF16)
        low = (stacked - high.astype(F32)).astype(BF16)
        found = (matmul(high, mean) + matmul(low, mean)) * (1.0 / (LOOK_AZ * LOOK_RG))
        return [found[i * looks : (i + 1) * looks] for i in range(len(sums))]

    def cross(a, b):
        return [a[0] * b[0] + a[1] * b[1], a[1] * b[0] - a[0] * b[1]]

    def power(a):
        return a[0] * a[0] + a[1] * a[1]

    def coherence(re, im, first, second):
        return jnp.sqrt(re * re + im * im) / jnp.sqrt(first * second + eps_power)

    def compare(s, carry):
        @pl.when(inner & jnp.logical_not(early_f))
        def _():
            pass_on(s, True, False)

        @pl.when(inner & jnp.logical_not(early_b))
        def _():
            pass_on(s, False, False)

        @pl.when(at_first)
        def _():
            line_copy(s, False).wait_recv()

        @pl.when(at_last)
        def _():
            line_copy(s, True).wait_recv()

        owner = owner_ref[s]

        def terms(l):
            def parts(read):
                return [
                    read(slice(p * rows + l * looks, p * rows + (l + 1) * looks)).astype(F32)
                    for p in range(2)
                ]

            images = [parts(lambda at, k=k: cur[s, k, at, :]) for k in range(scenes)]
            before = parts(lambda at: recv_f[s, at, :])
            after = parts(lambda at: recv_b[s, at, :])
            mine = parts(lambda at: own[s, at, :])
            ref = [
                jnp.where(owner == me, o, jnp.where(owner < me, f, b))
                for o, f, b in zip(mine, before, after)
            ]
            before = [jnp.where(at_first, r, f) for r, f in zip(ref, before)]
            chain = [before] + images + [after]
            out = []
            for image in images:
                out += cross(ref, image)
            for one, two in zip(chain[:-1], chain[1:]):
                out += cross(one, two)
            return out + [power(image) for image in chain]

        found = multilooked(row_sums(terms))
        pairs = found[: 2 * scenes]
        seqs = found[2 * scenes : 4 * scenes + 2]
        powers = found[4 * scenes + 2 :]
        at = pl.ds(pl.multiple_of(s * looks, looks), looks)
        for k in range(scenes + 1):
            re, im = seqs[2 * k], seqs[2 * k + 1]
            coherent = coherence(re, im, powers[k], powers[k + 1])
            if k < scenes:
                pair_ref[k, 0, at, :] = pairs[2 * k]
                pair_ref[k, 1, at, :] = pairs[2 * k + 1]
                seq_ref[k, 0, at, :] = re
                seq_ref[k, 1, at, :] = im
                coh_ref[k, at, :] = coherent
            else:
                for i, value in enumerate((re, im, coherent)):
                    ret_s[s, i] = value

        @pl.when(jnp.logical_not(at_last))
        def _():
            result_copy(s).start()

        return carry

    lax.fori_loop(0, tiles, compare, 0)

    def settle(s, carry):
        @pl.when(jnp.logical_not(at_first))
        def _():
            result_copy(s).wait_recv()
            returned = owner_ref[s] < me
            at = pl.ds(pl.multiple_of(s * looks, looks), looks)
            for p in range(2):
                seq_ref[0, p, at, :] = jnp.where(returned, ret_r[s, p], seq_ref[0, p, at, :])
            coh_ref[0, at, :] = jnp.where(returned, ret_r[s, 2], coh_ref[0, at, :])
            line_copy(s, False).wait_send()

        @pl.when(jnp.logical_not(at_last))
        def _():
            line_copy(s, True).wait_send()
            result_copy(s).wait_send()

        @pl.when(has_left)
        def _():
            edge_copy(s, 0).wait_send()

        @pl.when(has_right)
        def _():
            edge_copy(s, 1).wait_send()

        return carry

    lax.fori_loop(0, tiles, settle, 0)


def local(n_scene, n_range, *operands):
    secondary, store, _, az_kernel = operands[:4]
    scenes, length, parts, cols = secondary.shape
    _, tiles, rows = store.shape[:3]
    taps = az_kernel.shape[1]
    margin = (length - tiles * rows) // 2
    looks, cells = rows // LOOK_AZ, cols // LOOK_RG
    both = 2 * rows
    wide = -(-2 * (rows + 2 * margin) // LANES) * LANES
    image = (both, cols)
    dma = pltpu.SemaphoreType.DMA
    vmem = pl.BlockSpec(memory_space=pltpu.VMEM)
    hbm = pl.BlockSpec(memory_space=pl.ANY)
    smem = pl.BlockSpec(memory_space=pltpu.SMEM)
    strip = tiles * looks
    return pl.pallas_call(
        functools.partial(kernel_body, (scenes, tiles, rows, cols, margin, taps, n_scene, n_range)),
        out_shape=(
            jax.ShapeDtypeStruct((scenes, 2, strip, cells), F32),
            jax.ShapeDtypeStruct((scenes, 2, strip, cells), F32),
            jax.ShapeDtypeStruct((scenes, strip, cells), F32),
        ),
        in_specs=[hbm, hbm, smem] + [vmem] * 6,
        out_specs=(vmem, vmem, vmem),
        scratch_shapes=[
            pltpu.VMEM((scenes, 2 * length, cols), BF16),
            pltpu.VMEM((tiles,) + image, BF16),
            pltpu.VMEM((tiles,) + image, BF16),
            pltpu.VMEM((tiles, scenes) + image, BF16),
            pltpu.VMEM((tiles, scenes) + image, BF16),
            pltpu.VMEM((both, wide), BF16),
            pltpu.VMEM((scenes, cols, cols), BF16),
            pltpu.VMEM((scenes, 2 * margin, cols), BF16),
            pltpu.VMEM((az_kernel.shape[0] + 16, 2 * LANES), BF16),
            pltpu.VMEM((rows, rows), BF16),
            pltpu.VMEM((tiles, 2, scenes, margin, both), BF16),
            pltpu.VMEM((tiles, 2, scenes, margin, both), BF16),
            pltpu.VMEM((tiles,) + image, BF16),
            pltpu.VMEM((tiles,) + image, BF16),
            pltpu.VMEM((tiles,) + image, BF16),
            pltpu.VMEM((tiles,) + image, BF16),
            pltpu.VMEM((tiles, 3, looks, cells), F32),
            pltpu.VMEM((tiles, 3, looks, cells), F32),
            dma((scenes,)),
            dma((tiles,)),
            dma((tiles, 2)),
            dma((tiles, 2)),
            dma((tiles,)),
            dma((tiles,)),
            dma((tiles,)),
            dma((tiles,)),
            dma((tiles,)),
            dma((tiles,)),
        ],
        compiler_params=pltpu.CompilerParams(
            collective_id=0, has_side_effects=True, vmem_limit_bytes=48 << 20
        ),
    )(*operands)


def solution(mesh):
    in_specs = (
        P(("parts", "scene"), None, None, "range"),
        P(("parts", "scene"), None, None, None, "range"),
        P("parts"),
        P(),
        P(),
        P(("parts", "scene"), None),
        P(("parts", "scene"), None),
        P(("parts", "scene"), "range"),
        P(("parts", "scene"), "range"),
    )
    out_specs = (
        P(("parts", "scene"), None, None, "range"),
        P(("parts", "scene"), None, None, "range"),
        P(("parts", "scene"), None, "range"),
    )
    body = functools.partial(local, mesh.shape["scene"], mesh.shape["range"])
    return jax.shard_map(body, mesh=mesh, in_specs=in_specs, out_specs=out_specs, check_vma=False)
```

```python
import functools

import jax
import jax.numpy as jnp
from jax import lax
from jax.experimental import pallas as pl
from jax.experimental.pallas import tpu as pltpu
from jax.sharding import PartitionSpec as P

LOOK_AZ = 4
LOOK_RG = 16
LANES = 128
GROUP = 16
VMEM_BYTES = 62 << 20

eps_power = 1e-06
F32 = jnp.float32
BF16 = jnp.bfloat16
MESH = pl.DeviceIdType.MESH


def iota(shape, dim):
    return lax.broadcasted_iota(jnp.int32, shape, dim)


def flag(condition):
    return jnp.where(condition, 1.0, 0.0).astype(BF16)


def matmul(a, b, contract=((1,), (0,))):
    return lax.dot_general(a, b, (contract, ((), ())), preferred_element_type=F32)


def tap_table(kernel, stride):
    taps, count = kernel.shape
    place = flag(iota((taps, LANES), 1) == stride * iota((taps, LANES), 0))
    spread = matmul(kernel.astype(BF16), place, ((0,), (0,))).astype(BF16)
    ones = flag(iota((GROUP, LANES), 0) == 0)
    return jnp.concatenate(
        [
            jnp.concatenate([spread, jnp.zeros((count, LANES), BF16)], 1),
            jnp.concatenate([jnp.zeros((GROUP, LANES), BF16), ones], 1),
        ],
        0,
    )


def looked_up(table, index, offset):
    count = table.shape[0] - GROUP
    length = index.shape[1]
    one_hot = flag(iota((count, length), 0) == index)
    shift = jnp.broadcast_to(offset.astype(F32), (GROUP, length)).astype(BF16)
    return matmul(jnp.concatenate([one_hot, shift], 0), table, ((0,), (0,)))


def banded(taps, place, reach):
    if reach & (reach - 1):
        inside = (place >= 0) & (place < reach)
    else:
        inside = (place & -reach) == 0
    picked = jnp.take_along_axis(taps, place & (LANES - 1), axis=1, mode="promise_in_bounds")
    return jnp.where(inside, picked, 0.0).astype(BF16)


def cross(a, b):
    return [a[0] * b[0] + a[1] * b[1], a[1] * b[0] - a[0] * b[1]]


def power(a):
    return a[0] * a[0] + a[1] * a[1]


def coherence(re, im, first, second):
    return jnp.sqrt(re * re + im * im) / jnp.sqrt(first * second + eps_power)


def kernel_body(
    dims,
    sec_hbm, store_hbm, owner_hbm, azk_hbm, rgk_hbm, azo_hbm, azi_hbm, rgo_hbm, rgi_hbm,
    pair_ref, seq_ref, coh_ref,
    owner_ref, azk, rgk, azo, azi, rgo, rgi,
    sec, store, other, own, z, cur, az_mat, rg_mat, rg_halo, table, edge, halo,
    comm, relayed, y_send, ref, stats, packed, ret_s, ret_r,
    small_sem, sec_sem, store_sem, edge_sem, halo_sem, xs_sem, xr_sem, hs_sem, hr_sem,
    ys_sem, yr_sem, ls_sem, lr_sem, rs_sem, rr_sem,
):
    scenes, tiles, rows, cols, margin, taps, n_scene, n_range = dims
    looks = rows // LOOK_AZ
    both = 2 * rows
    deep = LOOK_AZ * GROUP
    blocks = rows // deep
    lines = 2 * (tiles * rows + 2 * margin)
    me = lax.axis_index("scene")
    col = lax.axis_index("range")
    core, chip = lax.rem(me, 2), lax.div(me, 2)
    is_l, is_r = core == 0, core == 1
    sibling = me + 1 - 2 * core
    outer = me - 1 + 2 * core
    has_prev, has_next = chip > 0, chip < n_scene // 2 - 1
    inner = has_prev & has_next
    l_up, r_up = is_l & has_prev, is_r & has_next
    has_outer = l_up | r_up
    has_left, has_right = col > 0, col < n_range - 1
    always = me >= 0
    sides = (
        (has_left, {"range": col - 1}),
        (has_right, {"range": col + 1}),
        (always, {"scene": sibling}),
        (has_outer, {"scene": outer}),
    )

    smalls = [
        pltpu.make_async_copy(source, target, small_sem.at[i])
        for i, (source, target) in enumerate(
            (
                (rgk_hbm, rgk), (rgo_hbm, rgo), (rgi_hbm, rgi), (azk_hbm, azk),
                (azo_hbm, azo), (azi_hbm, azi), (owner_hbm, owner_ref),
            )
        )
    ]

    def load_store(s):
        source = store_hbm.reshape(tiles, both, cols).at[s]
        return pltpu.make_async_copy(source, store.at[s], store_sem.at[s])

    def load_sec(k):
        source = sec_hbm.reshape(scenes, lines, cols).at[k]
        return pltpu.make_async_copy(source, sec.at[k, pl.ds(0, lines)], sec_sem.at[k])

    for copy in smalls:
        copy.start()
    for k in range(scenes):
        load_sec(k).start()
    for s in range(tiles):
        load_store(s).start()

    barrier = pltpu.get_barrier_semaphore()
    for exists, device in sides:
        @pl.when(exists)
        def _():
            pl.semaphore_signal(barrier, inc=1, device_id=device, device_id_type=MESH)

    @pl.when(jnp.logical_not(has_left))
    def _():
        halo[:, 0] = jnp.zeros(halo.shape[:1] + halo.shape[2:], BF16)

    @pl.when(jnp.logical_not(has_right))
    def _():
        halo[:, 1] = jnp.zeros(halo.shape[:1] + halo.shape[2:], BF16)

    def remote(source, target, sent, got, device):
        return pltpu.make_async_remote_copy(
            src_ref=source,
            dst_ref=target,
            send_sem=sent,
            recv_sem=got,
            device_id=device,
            device_id_type=MESH,
        )

    def edge_copy(s, side):
        return remote(
            edge.at[s, side],
            halo.at[s, 1 - side],
            edge_sem.at[s, side],
            halo_sem.at[s, 1 - side],
            {"range": col - 1 if side == 0 else col + 1},
        )

    def candidate_copy(s):
        return remote(store.at[s], other.at[s], xs_sem.at[s], xr_sem.at[s], {"scene": sibling})

    def handoff_copy(s):
        source = cur.at[s, scenes - 1]
        return remote(source, comm.at[0, s], hs_sem.at[s], hr_sem.at[s], {"scene": sibling})

    def line_copy(s):
        target = comm.at[1 - core, s]
        return remote(y_send.at[s], target, ys_sem.at[s], yr_sem.at[s], {"scene": outer})

    def relay_copy(s):
        source = comm.at[core, s]
        return remote(source, relayed.at[s], ls_sem.at[s], lr_sem.at[s], {"scene": sibling})

    def result_copy(s):
        return remote(ret_s.at[s], ret_r.at[s], rs_sem.at[s], rr_sem.at[s], {"scene": outer})

    for k in range(scenes):
        sec[k, lines:, :] = jnp.zeros((sec.shape[1] - lines, cols), BF16)

    for copy in smalls[:3]:
        copy.wait()
    rg_table = tap_table(rgk[...], 1)
    for k in range(scenes):
        found = looked_up(rg_table, rgi[k : k + 1, :], rgo[k : k + 1, :])
        tap_rows, shift = found[:, :LANES], found[:, LANES:].astype(jnp.int32)
        lane = iota((cols, LANES), 1)
        start = iota((cols, LANES), 0) + shift + (margin - 3)
        for t in range(cols // LANES):
            rg_mat[k, :, t * LANES : (t + 1) * LANES] = banded(
                tap_rows, lane + (t * LANES + margin) - start, taps
            )
        beside = jnp.where(lane < margin, lane, lane + cols)
        beside = jnp.where(lane < 2 * margin, beside, 4 * cols)
        outside = banded(tap_rows, beside - start, taps).astype(F32)
        rg_halo[k] = jnp.transpose(outside)[: 2 * margin].astype(BF16)
    for copy in smalls[3:]:
        copy.wait()
    table[...] = tap_table(azk[...], 2)

    def by_look(parts):
        shape = (parts, LOOK_AZ, GROUP, parts * deep)
        source = parts * (LOOK_AZ * iota(shape, 2) + iota(shape, 1)) + iota(shape, 0)
        return flag(iota(shape, 3) == source).reshape(parts * deep, parts * deep)

    def azimuth(s):
        order = by_look(1)
        for k in range(scenes):
            here = pl.ds(pl.multiple_of(s * rows, rows), rows)
            found = looked_up(table[...], azi[k : k + 1, here], azo[k : k + 1, here]).astype(BF16)
            for j in range(blocks):
                part = matmul(order, found[j * deep : (j + 1) * deep])
                tap_rows, shift = part[:, :LANES], part[:, LANES:].astype(jnp.int32)
                shape = (LOOK_AZ, GROUP, LANES)
                row = (LOOK_AZ * iota(shape, 1) + iota(shape, 0)).reshape(deep, LANES)
                start = iota((deep, LANES), 1) - 2 * (row + shift + (margin - 3))
                for p in range(2):
                    for t in range(2):
                        az_mat[
                            k, j, p * deep : (p + 1) * deep, t * LANES : (t + 1) * LANES
                        ] = banded(tap_rows, start + (t * LANES - p), 2 * taps)
            for j in range(blocks):
                first = pl.multiple_of(s * both + j * 2 * deep, 2 * deep)
                found = matmul(az_mat[k, j], sec[k, pl.ds(first, 2 * LANES), :])
                z[s, k, j * 2 * deep : (j + 1) * 2 * deep, :] = found.astype(BF16)
            which = iota((2 * margin, cols), 0)
            which = jnp.where(which < margin, which, which + cols - 2 * margin)
            ends = matmul(flag(iota((2 * margin, cols), 1) == which), z[s, k], ((1,), (1,)))
            ends = ends.astype(BF16)
            edge[s, 0, k] = ends[:margin]
            edge[s, 1, k] = ends[margin:]

        @pl.when(has_left)
        def _():
            edge_copy(s, 0).start()

        @pl.when(has_right)
        def _():
            edge_copy(s, 1).start()

    def range_step(s):
        @pl.when(has_left)
        def _():
            edge_copy(s, 1).wait_recv()

        @pl.when(has_right)
        def _():
            edge_copy(s, 0).wait_recv()

        for k in range(scenes):
            beside = jnp.concatenate([halo[s, 0, k], halo[s, 1, k]], 0)
            total = matmul(z[s, k], rg_mat[k], ((1,), (1,)))
            total = total + matmul(beside, rg_halo[k], ((0,), (0,)))
            cur[s, k] = total.astype(BF16)

    def line_send(s, from_relay):
        owner_chip = lax.div(owner_ref[s], 2)
        value = cur[s, core * (scenes - 1)]
        if from_relay:
            beyond = (is_r & (owner_chip < chip)) | (is_l & (owner_chip > chip))
            value = jnp.where(beyond, relayed[s], value)
        y_send[s] = jnp.where(owner_chip == chip, own[s], value)
        line_copy(s).start()

    pl.semaphore_wait(barrier, sum(exists.astype(jnp.int32) for exists, _ in sides))
    for s in range(tiles):
        load_store(s).wait()
        candidate_copy(s).start()
    for k in range(scenes):
        load_sec(k).wait()
    azimuth(0)

    def resample(s, carry):
        @pl.when(s + 1 < tiles)
        def _():
            azimuth(s + 1)

        range_step(s)

        @pl.when(is_l)
        def _():
            handoff_copy(s).start()

        candidate_copy(s).wait_recv()
        order = by_look(2)
        for j in range(blocks):
            at = slice(j * 2 * deep, (j + 1) * 2 * deep)
            chosen = jnp.where(owner_ref[s] == sibling, other[s, at, :], store[s, at, :])
            own[s, at, :] = matmul(order, chosen).astype(BF16)

        @pl.when(has_outer & jnp.logical_not(inner))
        def _():
            line_send(s, False)

        return carry

    lax.fori_loop(0, tiles, resample, 0)

    lane = iota((cols, LANES), 1) & (GROUP - 1)
    start = LOOK_RG * lane
    place = iota((cols, LANES), 0)
    mean = flag((place >= start) & (place < start + LOOK_RG))
    lane_group = iota((looks, LANES), 1)

    def multilooked(count, terms):
        sums = [[] for _ in range(count)]
        for j in range(blocks):
            total = None
            for l in range(LOOK_AZ):
                new = terms(j, l)
                total = new if total is None else [a + b for a, b in zip(total, new)]
            for one, value in zip(sums, total):
                one.append(value)
        stacked = jnp.concatenate([value for one in sums for value in one], 0)
        high = stacked.astype(BF16)
        low = (stacked - high.astype(F32)).astype(BF16)
        found = (matmul(high, mean) + matmul(low, mean)) * (1.0 / (LOOK_AZ * LOOK_RG))
        return [found[i * looks : (i + 1) * looks] for i in range(count)]

    def parts(read, j, l):
        first = j * 2 * deep + l * GROUP
        return [read(slice(first + p * deep, first + p * deep + GROUP)).astype(F32) for p in range(2)]

    def pack(values):
        out = values[-1]
        for i in range(len(values) - 2, -1, -1):
            out = jnp.where(lane_group < (i + 1) * GROUP, values[i], out)
        return out

    def own_terms(s, carry):
        def terms(j, l):
            images = [parts(lambda at, k=k: cur[s, k, at, :], j, l) for k in range(scenes)]
            out = [power(image) for image in images]
            for one, two in zip(images[:-1], images[1:]):
                out += cross(one, two)
            return out

        found = multilooked(scenes + 2 * (scenes - 1), terms)
        for i, value in enumerate(found):
            stats[s, i] = value
        return carry

    lax.fori_loop(0, tiles, own_terms, 0)

    def compare(s, carry):
        def arrived():
            line_copy(s).wait_recv()
            relay_copy(s).start()

        def handed():
            relay_copy(s).wait_recv()

            @pl.when(inner)
            def _():
                line_send(s, True)

        pl.when(l_up)(arrived)
        pl.when(is_r & has_prev)(handed)
        pl.when(r_up)(arrived)
        pl.when(is_l & has_next)(handed)

        @pl.when(is_r)
        def _():
            handoff_copy(s).wait_recv()

        @pl.when(r_up)
        def _():
            def terms(j, l):
                last = parts(lambda at: cur[s, scenes - 1, at, :], j, l)
                after = parts(lambda at: comm[1, s, at, :], j, l)
                return cross(last, after) + [power(after)]

            re, im, strength = multilooked(3, terms)
            coherent = coherence(re, im, stats[s, scenes - 1], strength)
            ret_s[s] = pack([re, im, re, im, coherent])
            result_copy(s).start()

        owner_chip = lax.div(owner_ref[s], 2)
        direct = (is_l & (owner_chip < chip)) | (is_r & (owner_chip > chip))
        far = jnp.where(direct, comm[core, s], relayed[s])
        ref[...] = jnp.where(owner_chip == chip, own[s], far)

        @pl.when(me == 0)
        def _():
            comm[0, s] = ref[...]

        def terms(j, l):
            images = [parts(lambda at, k=k: cur[s, k, at, :], j, l) for k in range(scenes)]
            given = parts(lambda at: ref[at, :], j, l)
            before = parts(lambda at: comm[0, s, at, :], j, l)
            out = cross(before, images[0]) + [power(before)]
            for image in images:
                out += cross(given, image)
            return out

        found = multilooked(3 + 2 * scenes, terms)
        strength = found[2]
        for k in range(scenes):
            if k == 0:
                re, im = found[0], found[1]
            else:
                re, im = stats[s, scenes + 2 * (k - 1)], stats[s, scenes + 2 * (k - 1) + 1]
            coherent = coherence(re, im, strength, stats[s, k])
            strength = stats[s, k]
            packed[k, s] = pack([found[3 + 2 * k], found[4 + 2 * k], re, im, coherent])
        return carry

    lax.fori_loop(0, tiles, compare, 0)

    def settle(s, carry):
        @pl.when(l_up)
        def _():
            result_copy(s).wait_recv()
            returned = (lax.div(owner_ref[s], 2) < chip) & (lane_group >= 2 * GROUP)
            packed[0, s] = jnp.where(returned, ret_r[s], packed[0, s])

        return carry

    lax.fori_loop(0, tiles, settle, 0)
    for k in range(scenes):
        planes = jnp.transpose(packed[k].reshape(tiles * looks, LANES))
        planes = [planes[i * GROUP : (i + 1) * GROUP] for i in range(5)]
        pair_ref[k, 0], pair_ref[k, 1], seq_ref[k, 0], seq_ref[k, 1], coh_ref[k] = planes

    def finish(s, carry):
        candidate_copy(s).wait_send()

        @pl.when(is_l)
        def _():
            handoff_copy(s).wait_send()

        @pl.when(has_outer)
        def _():
            line_copy(s).wait_send()
            relay_copy(s).wait_send()

        @pl.when(r_up)
        def _():
            result_copy(s).wait_send()

        @pl.when(has_left)
        def _():
            edge_copy(s, 0).wait_send()

        @pl.when(has_right)
        def _():
            edge_copy(s, 1).wait_send()

        return carry

    lax.fori_loop(0, tiles, finish, 0)


def local(n_scene, n_range, *operands):
    secondary, store, owner, az_kernel, rg_kernel = operands[:5]
    operands = operands[:3] + (az_kernel.T, rg_kernel.T) + operands[5:]
    scenes, length, _, cols = secondary.shape
    _, tiles, rows = store.shape[:3]
    count, taps = az_kernel.shape
    margin = (length - tiles * rows) // 2
    looks, cells = rows // LOOK_AZ, cols // LOOK_RG
    deep = LOOK_AZ * GROUP
    both = 2 * rows
    image = (both, cols)
    strip = tiles * looks
    dma = pltpu.SemaphoreType.DMA
    vmem = pltpu.VMEM
    home = pl.BlockSpec(memory_space=vmem)
    hbm = pl.BlockSpec(memory_space=pl.ANY)
    dims = (scenes, tiles, rows, cols, margin, taps, n_scene, n_range)
    pairs, sequential, coherent = pl.pallas_call(
        functools.partial(kernel_body, dims),
        out_shape=(
            jax.ShapeDtypeStruct((scenes, 2, cells, strip), F32),
            jax.ShapeDtypeStruct((scenes, 2, cells, strip), F32),
            jax.ShapeDtypeStruct((scenes, cells, strip), F32),
        ),
        in_specs=[hbm] * len(operands),
        out_specs=(home, home, home),
        scratch_shapes=[
            pltpu.SMEM(owner.shape, jnp.int32),
            vmem((taps, count), F32),
            vmem((taps, count), F32),
            vmem((scenes, tiles * rows), jnp.int32),
            vmem((scenes, tiles * rows), jnp.int32),
            vmem((scenes, cols), jnp.int32),
            vmem((scenes, cols), jnp.int32),
            vmem((scenes, 2 * (tiles * rows - deep + LANES), cols), BF16),
            vmem((tiles,) + image, BF16),
            vmem((tiles,) + image, BF16),
            vmem((tiles,) + image, BF16),
            vmem((tiles, scenes) + image, BF16),
            vmem((tiles, scenes) + image, BF16),
            vmem((scenes, rows // deep, 2 * deep, 2 * LANES), BF16),
            vmem((scenes, cols, cols), BF16),
            vmem((scenes, 2 * margin, cols), BF16),
            vmem((count + GROUP, 2 * LANES), BF16),
            vmem((tiles, 2, scenes, margin, both), BF16),
            vmem((tiles, 2, scenes, margin, both), BF16),
            vmem((2, tiles) + image, BF16),
            vmem((tiles,) + image, BF16),
            vmem((tiles,) + image, BF16),
            vmem(image, BF16),
            vmem((tiles, scenes + 2 * (scenes - 1), looks, LANES), F32),
            vmem((scenes, tiles, looks, LANES), F32),
            vmem((tiles, looks, LANES), F32),
            vmem((tiles, looks, LANES), F32),
            dma((7,)),
            dma((scenes,)),
            dma((tiles,)),
            dma((tiles, 2)),
            dma((tiles, 2)),
        ]
        + [dma((tiles,))] * 10,
        compiler_params=pltpu.CompilerParams(
            collective_id=0, has_side_effects=True, vmem_limit_bytes=VMEM_BYTES
        ),
    )(*operands)
    return tuple(jnp.swapaxes(value, -1, -2) for value in (pairs, sequential, coherent))


def solution(mesh):
    in_specs = (
        P(("parts", "scene"), None, None, "range"),
        P(("parts", "scene"), None, None, None, "range"),
        P("parts"),
        P(),
        P(),
        P(("parts", "scene"), None),
        P(("parts", "scene"), None),
        P(("parts", "scene"), "range"),
        P(("parts", "scene"), "range"),
    )
    out_specs = (
        P(("parts", "scene"), None, None, "range"),
        P(("parts", "scene"), None, None, "range"),
        P(("parts", "scene"), None, "range"),
    )
    body = functools.partial(local, mesh.shape["scene"], mesh.shape["range"])
    return jax.shard_map(body, mesh=mesh, in_specs=in_specs, out_specs=out_specs, check_vma=False)
```

```python
import functools

import jax
import jax.numpy as jnp
from jax import lax
from jax.experimental import pallas as pl
from jax.experimental.pallas import tpu as pltpu
from jax.sharding import PartitionSpec as P

LOOK_AZ = 4
LOOK_RG = 16
LANES = 128
GROUP = 16
VMEM_BYTES = 32 << 20

eps_power = 1e-06
F32 = jnp.float32
BF16 = jnp.bfloat16
MESH = pl.DeviceIdType.MESH


def iota(shape, dim):
    return lax.broadcasted_iota(jnp.int32, shape, dim)


def flag(condition):
    return jnp.where(condition, 1.0, 0.0).astype(BF16)


def matmul(a, b, contract=((1,), (0,))):
    return lax.dot_general(a, b, (contract, ((), ())), preferred_element_type=F32)


def tap_table(kernel, stride):
    taps, count = kernel.shape
    place = flag(iota((taps, LANES), 1) == stride * iota((taps, LANES), 0))
    spread = matmul(kernel.astype(BF16), place, ((0,), (0,))).astype(BF16)
    ones = flag(iota((GROUP, LANES), 0) == 0)
    return jnp.concatenate(
        [
            jnp.concatenate([spread, jnp.zeros((count, LANES), BF16)], 1),
            jnp.concatenate([jnp.zeros((GROUP, LANES), BF16), ones], 1),
        ],
        0,
    )


def looked_up(table, index, offset):
    count = table.shape[0] - GROUP
    length = index.shape[1]
    one_hot = flag(iota((count, length), 0) == index)
    shift = jnp.broadcast_to(offset.astype(F32), (GROUP, length)).astype(BF16)
    return matmul(jnp.concatenate([one_hot, shift], 0), table, ((0,), (0,)))


def banded(taps, place, reach):
    if reach & (reach - 1):
        inside = (place >= 0) & (place < reach)
    else:
        inside = (place & -reach) == 0
    picked = jnp.take_along_axis(taps, place & (LANES - 1), axis=1, mode="promise_in_bounds")
    return jnp.where(inside, picked, 0.0).astype(BF16)


def cross(a, b):
    return [a[0] * b[0] + a[1] * b[1], a[1] * b[0] - a[0] * b[1]]


def power(a):
    return a[0] * a[0] + a[1] * a[1]


def coherence(re, im, first, second):
    return jnp.sqrt(re * re + im * im) / jnp.sqrt(first * second + eps_power)


def kernel_body(
    dims,
    sec_hbm, store_hbm, owner_hbm, azk_hbm, rgk_hbm, azo_hbm, azi_hbm, rgo_hbm, rgi_hbm,
    pair_ref, seq_ref, coh_ref,
    owner_ref, azk, rgk, azo, azi, rgo, rgi,
    sec, store, other, own, z, cur, az_mat, rg_mat, rg_halo, table, edge, halo,
    comm, relayed, y_send, ref, stats, packed, ret_s, ret_r,
    small_sem, sec_sem, store_sem, edge_sem, halo_sem, xs_sem, xr_sem, hs_sem, hr_sem,
    ys_sem, yr_sem, ls_sem, lr_sem, rs_sem, rr_sem,
):
    scenes, tiles, rows, cols, margin, taps, n_scene, n_range = dims
    looks = rows // LOOK_AZ
    both = 2 * rows
    deep = LOOK_AZ * GROUP
    blocks = rows // deep
    lines = 2 * (tiles * rows + 2 * margin)
    me = lax.axis_index("scene")
    col = lax.axis_index("range")
    core, chip = lax.rem(me, 2), lax.div(me, 2)
    is_l, is_r = core == 0, core == 1
    sibling = me + 1 - 2 * core
    outer = me - 1 + 2 * core
    has_prev, has_next = chip > 0, chip < n_scene // 2 - 1
    inner = has_prev & has_next
    l_up, r_up = is_l & has_prev, is_r & has_next
    has_outer = l_up | r_up
    has_left, has_right = col > 0, col < n_range - 1
    always = me >= 0
    sides = (
        (has_left, {"range": col - 1}),
        (has_right, {"range": col + 1}),
        (always, {"scene": sibling}),
        (has_outer, {"scene": outer}),
    )

    smalls = [
        pltpu.make_async_copy(source, target, small_sem.at[i])
        for i, (source, target) in enumerate(
            (
                (azk_hbm, azk), (azo_hbm, azo), (azi_hbm, azi), (rgk_hbm, rgk),
                (rgo_hbm, rgo), (rgi_hbm, rgi), (owner_hbm, owner_ref),
            )
        )
    ]

    def load_store(s):
        source = store_hbm.reshape(tiles, both, cols).at[s]
        return pltpu.make_async_copy(source, store.at[s], store_sem.at[s])

    def load_sec(k, s):
        first, end = (
            0 if t < 0 else min(lines, (t + 1) * both - 2 * deep + 2 * LANES) for t in (s - 1, s)
        )
        length = end - first
        source = sec_hbm.at[k, pl.ds(first // 2, length // 2)].reshape(length, cols)
        return pltpu.make_async_copy(source, sec.at[k, pl.ds(first, length)], sec_sem.at[k, s])

    for copy in smalls:
        copy.start()
    for s in range(tiles):
        for k in range(scenes):
            load_sec(k, s).start()
        load_store(s).start()

    barrier = pltpu.get_barrier_semaphore()
    for exists, device in sides:
        @pl.when(exists)
        def _():
            pl.semaphore_signal(barrier, inc=1, device_id=device, device_id_type=MESH)

    @pl.when(jnp.logical_not(has_left))
    def _():
        halo[:, 0] = jnp.zeros(halo.shape[:1] + halo.shape[2:], BF16)

    @pl.when(jnp.logical_not(has_right))
    def _():
        halo[:, 1] = jnp.zeros(halo.shape[:1] + halo.shape[2:], BF16)

    def remote(source, target, sent, got, device):
        return pltpu.make_async_remote_copy(
            src_ref=source,
            dst_ref=target,
            send_sem=sent,
            recv_sem=got,
            device_id=device,
            device_id_type=MESH,
        )

    def edge_copy(s, side):
        return remote(
            edge.at[s, side],
            halo.at[s, 1 - side],
            edge_sem.at[s, side],
            halo_sem.at[s, 1 - side],
            {"range": col - 1 if side == 0 else col + 1},
        )

    def candidate_copy(s):
        return remote(store.at[s], other.at[s], xs_sem.at[s], xr_sem.at[s], {"scene": sibling})

    def handoff_copy(s):
        source = cur.at[s, scenes - 1]
        return remote(source, comm.at[0, s], hs_sem.at[s], hr_sem.at[s], {"scene": sibling})

    def line_copy(s):
        target = comm.at[1 - core, s]
        return remote(y_send.at[s], target, ys_sem.at[s], yr_sem.at[s], {"scene": outer})

    def relay_copy(s):
        source = comm.at[core, s]
        return remote(source, relayed.at[s], ls_sem.at[s], lr_sem.at[s], {"scene": sibling})

    def result_copy(s):
        return remote(ret_s.at[s], ret_r.at[s], rs_sem.at[s], rr_sem.at[s], {"scene": outer})

    for k in range(scenes):
        sec[k, lines:, :] = jnp.zeros((sec.shape[1] - lines, cols), BF16)

    for copy in smalls[:3]:
        copy.wait()
    table[...] = tap_table(azk[...], 2)

    def by_look(parts):
        shape = (parts, LOOK_AZ, GROUP, parts * deep)
        source = parts * (LOOK_AZ * iota(shape, 2) + iota(shape, 1)) + iota(shape, 0)
        return flag(iota(shape, 3) == source).reshape(parts * deep, parts * deep)

    def azimuth(s):
        order = by_look(1)
        for k in range(scenes):
            here = pl.ds(pl.multiple_of(s * rows, rows), rows)
            found = looked_up(table[...], azi[k : k + 1, here], azo[k : k + 1, here]).astype(BF16)
            for j in range(blocks):
                part = matmul(order, found[j * deep : (j + 1) * deep])
                tap_rows, shift = part[:, :LANES], part[:, LANES:].astype(jnp.int32)
                shape = (LOOK_AZ, GROUP, LANES)
                row = (LOOK_AZ * iota(shape, 1) + iota(shape, 0)).reshape(deep, LANES)
                start = iota((deep, LANES), 1) - 2 * (row + shift + (margin - 3))
                for p in range(2):
                    for t in range(2):
                        az_mat[
                            k, j, p * deep : (p + 1) * deep, t * LANES : (t + 1) * LANES
                        ] = banded(tap_rows, start + (t * LANES - p), 2 * taps)
            for j in range(blocks):
                first = pl.multiple_of(s * both + j * 2 * deep, 2 * deep)
                found = matmul(az_mat[k, j], sec[k, pl.ds(first, 2 * LANES), :])
                z[s, k, j * 2 * deep : (j + 1) * 2 * deep, :] = found.astype(BF16)
            which = iota((2 * margin, cols), 0)
            which = jnp.where(which < margin, which, which + cols - 2 * margin)
            ends = matmul(flag(iota((2 * margin, cols), 1) == which), z[s, k], ((1,), (1,)))
            ends = ends.astype(BF16)
            edge[s, 0, k] = ends[:margin]
            edge[s, 1, k] = ends[margin:]

    def send_edges(s):
        @pl.when(has_left)
        def _():
            edge_copy(s, 0).start()

        @pl.when(has_right)
        def _():
            edge_copy(s, 1).start()

    def range_step(s):
        @pl.when(has_left)
        def _():
            edge_copy(s, 1).wait_recv()

        @pl.when(has_right)
        def _():
            edge_copy(s, 0).wait_recv()

        for k in range(scenes):
            beside = jnp.concatenate([halo[s, 0, k], halo[s, 1, k]], 0)
            total = matmul(z[s, k], rg_mat[k], ((1,), (1,)))
            total = total + matmul(beside, rg_halo[k], ((0,), (0,)))
            cur[s, k] = total.astype(BF16)

    def line_send(s, from_relay):
        owner_chip = lax.div(owner_ref[s], 2)
        value = cur[s, core * (scenes - 1)]
        if from_relay:
            beyond = (is_r & (owner_chip < chip)) | (is_l & (owner_chip > chip))
            value = jnp.where(beyond, relayed[s], value)
        y_send[s] = jnp.where(owner_chip == chip, own[s], value)
        line_copy(s).start()

    lane = iota((cols, LANES), 1) & (GROUP - 1)
    start = LOOK_RG * lane
    place = iota((cols, LANES), 0)
    mean = flag((place >= start) & (place < start + LOOK_RG))
    lane_group = iota((looks, LANES), 1)

    def multilooked(count, terms):
        sums = [[] for _ in range(count)]
        for j in range(blocks):
            total = None
            for l in range(LOOK_AZ):
                new = terms(j, l)
                total = new if total is None else [a + b for a, b in zip(total, new)]
            for one, value in zip(sums, total):
                one.append(value)
        stacked = jnp.concatenate([value for one in sums for value in one], 0)
        high = stacked.astype(BF16)
        low = (stacked - high.astype(F32)).astype(BF16)
        found = (matmul(high, mean) + matmul(low, mean)) * (1.0 / (LOOK_AZ * LOOK_RG))
        return [found[i * looks : (i + 1) * looks] for i in range(count)]

    def parts(read, j, l):
        first = j * 2 * deep + l * GROUP
        return [read(slice(first + p * deep, first + p * deep + GROUP)).astype(F32) for p in range(2)]

    def pack(values):
        out = values[-1]
        for i in range(len(values) - 2, -1, -1):
            out = jnp.where(lane_group < (i + 1) * GROUP, values[i], out)
        return out

    def own_terms(s):
        def terms(j, l):
            images = [parts(lambda at, k=k: cur[s, k, at, :], j, l) for k in range(scenes)]
            out = [power(image) for image in images]
            for one, two in zip(images[:-1], images[1:]):
                out += cross(one, two)
            return out

        found = multilooked(scenes + 2 * (scenes - 1), terms)
        for i, value in enumerate(found):
            stats[s, i] = value

    for k in range(scenes):
        load_sec(k, 0).wait()
    azimuth(0)
    pl.semaphore_wait(barrier, sum(exists.astype(jnp.int32) for exists, _ in sides))
    send_edges(0)
    for s in range(tiles):
        load_store(s).wait()
        candidate_copy(s).start()

    for copy in smalls[3:]:
        copy.wait()
    rg_table = tap_table(rgk[...], 1)
    for k in range(scenes):
        found = looked_up(rg_table, rgi[k : k + 1, :], rgo[k : k + 1, :])
        tap_rows, shift = found[:, :LANES], found[:, LANES:].astype(jnp.int32)
        lane = iota((cols, LANES), 1)
        start = iota((cols, LANES), 0) + shift + (margin - 3)
        for t in range(cols // LANES):
            rg_mat[k, :, t * LANES : (t + 1) * LANES] = banded(
                tap_rows, lane + (t * LANES + margin) - start, taps
            )
        beside = jnp.where(lane < margin, lane, lane + cols)
        beside = jnp.where(lane < 2 * margin, beside, 4 * cols)
        outside = banded(tap_rows, beside - start, taps).astype(F32)
        rg_halo[k] = jnp.transpose(outside)[: 2 * margin].astype(BF16)

    def resample(s, more):
        candidate_copy(s).wait_recv()
        order = by_look(2)
        for j in range(blocks):
            at = slice(j * 2 * deep, (j + 1) * 2 * deep)
            chosen = jnp.where(owner_ref[s] == sibling, other[s, at, :], store[s, at, :])
            own[s, at, :] = matmul(order, chosen).astype(BF16)
        range_step(s)

        @pl.when(has_outer & jnp.logical_not(inner))
        def _():
            line_send(s, False)

        @pl.when(is_l)
        def _():
            handoff_copy(s).start()

        if more:
            azimuth(s + 1)
            send_edges(s + 1)
        own_terms(s)

    def resample_step(s, carry):
        resample(s, True)
        return carry

    for s in range(1, tiles):
        for k in range(scenes):
            load_sec(k, s).wait()
    lax.fori_loop(0, tiles - 1, resample_step, 0)
    resample(tiles - 1, False)

    def compare(s, carry):
        def arrived():
            line_copy(s).wait_recv()
            relay_copy(s).start()

        def handed():
            relay_copy(s).wait_recv()

            @pl.when(inner)
            def _():
                line_send(s, True)

        pl.when(l_up)(arrived)
        pl.when(is_r & has_prev)(handed)
        pl.when(r_up)(arrived)
        pl.when(is_l & has_next)(handed)

        @pl.when(is_r)
        def _():
            handoff_copy(s).wait_recv()

        @pl.when(r_up)
        def _():
            def terms(j, l):
                last = parts(lambda at: cur[s, scenes - 1, at, :], j, l)
                after = parts(lambda at: comm[1, s, at, :], j, l)
                return cross(last, after) + [power(after)]

            re, im, strength = multilooked(3, terms)
            coherent = coherence(re, im, stats[s, scenes - 1], strength)
            ret_s[s] = pack([re, im, re, im, coherent])
            result_copy(s).start()

        owner_chip = lax.div(owner_ref[s], 2)
        direct = (is_l & (owner_chip < chip)) | (is_r & (owner_chip > chip))
        far = jnp.where(direct, comm[core, s], relayed[s])
        ref[...] = jnp.where(owner_chip == chip, own[s], far)

        @pl.when(me == 0)
        def _():
            comm[0, s] = ref[...]

        def terms(j, l):
            images = [parts(lambda at, k=k: cur[s, k, at, :], j, l) for k in range(scenes)]
            given = parts(lambda at: ref[at, :], j, l)
            before = parts(lambda at: comm[0, s, at, :], j, l)
            out = cross(before, images[0]) + [power(before)]
            for image in images:
                out += cross(given, image)
            return out

        found = multilooked(3 + 2 * scenes, terms)
        strength = found[2]
        for k in range(scenes):
            if k == 0:
                re, im = found[0], found[1]
            else:
                re, im = stats[s, scenes + 2 * (k - 1)], stats[s, scenes + 2 * (k - 1) + 1]
            coherent = coherence(re, im, strength, stats[s, k])
            strength = stats[s, k]
            packed[k, s] = pack([found[3 + 2 * k], found[4 + 2 * k], re, im, coherent])
        return carry

    lax.fori_loop(0, tiles, compare, 0)

    def settle(s, carry):
        @pl.when(l_up)
        def _():
            result_copy(s).wait_recv()
            returned = (lax.div(owner_ref[s], 2) < chip) & (lane_group >= 2 * GROUP)
            packed[0, s] = jnp.where(returned, ret_r[s], packed[0, s])

        return carry

    lax.fori_loop(0, tiles, settle, 0)
    for k in range(scenes):
        planes = jnp.transpose(packed[k].reshape(tiles * looks, LANES))
        planes = [planes[i * GROUP : (i + 1) * GROUP] for i in range(5)]
        pair_ref[k, 0], pair_ref[k, 1], seq_ref[k, 0], seq_ref[k, 1], coh_ref[k] = planes

    def finish(s, carry):
        candidate_copy(s).wait_send()

        @pl.when(is_l)
        def _():
            handoff_copy(s).wait_send()

        @pl.when(has_outer)
        def _():
            line_copy(s).wait_send()
            relay_copy(s).wait_send()

        @pl.when(r_up)
        def _():
            result_copy(s).wait_send()

        @pl.when(has_left)
        def _():
            edge_copy(s, 0).wait_send()

        @pl.when(has_right)
        def _():
            edge_copy(s, 1).wait_send()

        return carry

    lax.fori_loop(0, tiles, finish, 0)


def write_out(*refs):
    count = len(refs) // 2
    copies = [
        pltpu.make_async_copy(refs[i], refs[count + i], refs[-1].at[i]) for i in range(count)
    ]
    for copy in copies:
        copy.start()
    for copy in copies:
        copy.wait()


def local(n_scene, n_range, *operands):
    secondary, store, owner, az_kernel, rg_kernel = operands[:5]
    operands = operands[:3] + (az_kernel.T, rg_kernel.T) + operands[5:]
    operands = [pltpu.with_memory_space_constraint(value, pltpu.HBM) for value in operands]
    scenes, length, _, cols = secondary.shape
    _, tiles, rows = store.shape[:3]
    count, taps = az_kernel.shape
    margin = (length - tiles * rows) // 2
    looks, cells = rows // LOOK_AZ, cols // LOOK_RG
    deep = LOOK_AZ * GROUP
    both = 2 * rows
    image = (both, cols)
    strip = tiles * looks
    dma = pltpu.SemaphoreType.DMA
    vmem = pltpu.VMEM
    home = pl.BlockSpec(memory_space=vmem)
    hbm = pl.BlockSpec(memory_space=pltpu.HBM)
    dims = (scenes, tiles, rows, cols, margin, taps, n_scene, n_range)
    results = pl.pallas_call(
        functools.partial(kernel_body, dims),
        out_shape=(
            jax.ShapeDtypeStruct((scenes, 2, cells, strip), F32),
            jax.ShapeDtypeStruct((scenes, 2, cells, strip), F32),
            jax.ShapeDtypeStruct((scenes, cells, strip), F32),
        ),
        in_specs=[hbm] * len(operands),
        out_specs=(home, home, home),
        scratch_shapes=[
            pltpu.SMEM(owner.shape, jnp.int32),
            vmem((taps, count), F32),
            vmem((taps, count), F32),
            vmem((scenes, tiles * rows), jnp.int32),
            vmem((scenes, tiles * rows), jnp.int32),
            vmem((scenes, cols), jnp.int32),
            vmem((scenes, cols), jnp.int32),
            vmem((scenes, 2 * (tiles * rows - deep + LANES), cols), BF16),
            vmem((tiles,) + image, BF16),
            vmem((tiles,) + image, BF16),
            vmem((tiles,) + image, BF16),
            vmem((tiles, scenes) + image, BF16),
            vmem((tiles, scenes) + image, BF16),
            vmem((scenes, rows // deep, 2 * deep, 2 * LANES), BF16),
            vmem((scenes, cols, cols), BF16),
            vmem((scenes, 2 * margin, cols), BF16),
            vmem((count + GROUP, 2 * LANES), BF16),
            vmem((tiles, 2, scenes, margin, both), BF16),
            vmem((tiles, 2, scenes, margin, both), BF16),
            vmem((2, tiles) + image, BF16),
            vmem((tiles,) + image, BF16),
            vmem((tiles,) + image, BF16),
            vmem(image, BF16),
            vmem((tiles, scenes + 2 * (scenes - 1), looks, LANES), F32),
            vmem((scenes, tiles, looks, LANES), F32),
            vmem((tiles, looks, LANES), F32),
            vmem((tiles, looks, LANES), F32),
            dma((7,)),
            dma((scenes, tiles)),
            dma((tiles,)),
            dma((tiles, 2)),
            dma((tiles, 2)),
        ]
        + [dma((tiles,))] * 10,
        compiler_params=pltpu.CompilerParams(
            collective_id=0, has_side_effects=True, vmem_limit_bytes=VMEM_BYTES
        ),
    )(*operands)
    results = pl.pallas_call(
        write_out,
        out_shape=[jax.ShapeDtypeStruct(value.shape, F32) for value in results],
        in_specs=[home] * len(results),
        out_specs=[hbm] * len(results),
        scratch_shapes=[dma((len(results),))],
    )(*results)
    return tuple(jnp.swapaxes(value, -1, -2) for value in results)


def solution(mesh):
    in_specs = (
        P(("parts", "scene"), None, None, "range"),
        P(("parts", "scene"), None, None, None, "range"),
        P("parts"),
        P(),
        P(),
        P(("parts", "scene"), None),
        P(("parts", "scene"), None),
        P(("parts", "scene"), "range"),
        P(("parts", "scene"), "range"),
    )
    out_specs = (
        P(("parts", "scene"), None, None, "range"),
        P(("parts", "scene"), None, None, "range"),
        P(("parts", "scene"), None, "range"),
    )
    body = functools.partial(local, mesh.shape["scene"], mesh.shape["range"])
    return jax.shard_map(body, mesh=mesh, in_specs=in_specs, out_specs=out_specs, check_vma=False)
```

```python
import functools

import jax
import jax.numpy as jnp
from jax import lax
from jax.experimental import pallas as pl
from jax.experimental.pallas import tpu as pltpu
from jax.sharding import PartitionSpec as P

LOOK_AZ = 4
LOOK_RG = 16
LANES = 128
GROUP = 16
EARLY = 2
VMEM_BYTES = 32 << 20

eps_power = 1e-06
F32 = jnp.float32
BF16 = jnp.bfloat16
MESH = pl.DeviceIdType.MESH


def iota(shape, dim):
    return lax.broadcasted_iota(jnp.int32, shape, dim)


def flag(condition):
    return jnp.where(condition, 1.0, 0.0).astype(BF16)


def matmul(a, b, contract=((1,), (0,))):
    return lax.dot_general(a, b, (contract, ((), ())), preferred_element_type=F32)


def tap_table(kernel, stride):
    taps, count = kernel.shape
    place = flag(iota((taps, LANES), 1) == stride * iota((taps, LANES), 0))
    spread = matmul(kernel.astype(BF16), place, ((0,), (0,))).astype(BF16)
    ones = flag(iota((GROUP, LANES), 0) == 0)
    return jnp.concatenate(
        [
            jnp.concatenate([spread, jnp.zeros((count, LANES), BF16)], 1),
            jnp.concatenate([jnp.zeros((GROUP, LANES), BF16), ones], 1),
        ],
        0,
    )


def looked_up(table, index, offset):
    count = table.shape[0] - GROUP
    length = index.shape[1]
    one_hot = flag(iota((count, length), 0) == index)
    shift = jnp.broadcast_to(offset.astype(F32), (GROUP, length)).astype(BF16)
    return matmul(jnp.concatenate([one_hot, shift], 0), table, ((0,), (0,)))


def banded(taps, place, reach):
    if reach & (reach - 1):
        inside = (place >= 0) & (place < reach)
    else:
        inside = (place & -reach) == 0
    picked = jnp.take_along_axis(taps, place & (LANES - 1), axis=1, mode="promise_in_bounds")
    return jnp.where(inside, picked, 0.0).astype(BF16)


def cross(a, b):
    return [a[0] * b[0] + a[1] * b[1], a[1] * b[0] - a[0] * b[1]]


def power(a):
    return a[0] * a[0] + a[1] * a[1]


def coherence(re, im, first, second):
    return jnp.sqrt(re * re + im * im) / jnp.sqrt(first * second + eps_power)


def kernel_body(
    dims,
    sec_hbm, store_hbm, owner_hbm, azk_hbm, rgk_hbm, azo_hbm, azi_hbm, rgo_hbm, rgi_hbm,
    pair_ref, seq_ref, coh_ref,
    owner_ref, azk, rgk, azo, azi, rgo, rgi,
    sec, store, other, own, z, cur, az_mat, rg_mat, rg_halo, table, edge, halo,
    comm, relayed, y_send, ref, stats, packed, ret_s, ret_r,
    small_sem, sec_sem, store_sem, edge_sem, halo_sem, xs_sem, xr_sem, hs_sem, hr_sem,
    ys_sem, yr_sem, ls_sem, lr_sem, rs_sem, rr_sem,
):
    scenes, tiles, rows, cols, margin, taps, n_scene, n_range = dims
    looks = rows // LOOK_AZ
    both = 2 * rows
    deep = LOOK_AZ * GROUP
    blocks = rows // deep
    lines = 2 * (tiles * rows + 2 * margin)
    me = lax.axis_index("scene")
    col = lax.axis_index("range")
    core, chip = lax.rem(me, 2), lax.div(me, 2)
    is_l, is_r = core == 0, core == 1
    sibling = me + 1 - 2 * core
    outer = me - 1 + 2 * core
    has_prev, has_next = chip > 0, chip < n_scene // 2 - 1
    inner = has_prev & has_next
    l_up, r_up = is_l & has_prev, is_r & has_next
    has_outer = l_up | r_up
    has_left, has_right = col > 0, col < n_range - 1
    always = me >= 0
    sides = (
        (has_left, {"range": col - 1}),
        (has_right, {"range": col + 1}),
        (always, {"scene": sibling}),
        (has_outer, {"scene": outer}),
    )

    smalls = [
        pltpu.make_async_copy(source, target, small_sem.at[i])
        for i, (source, target) in enumerate(
            (
                (azk_hbm, azk), (azo_hbm, azo), (azi_hbm, azi), (rgk_hbm, rgk),
                (rgo_hbm, rgo), (rgi_hbm, rgi), (owner_hbm, owner_ref),
            )
        )
    ]

    def load_store(s):
        source = store_hbm.reshape(tiles, both, cols).at[s]
        return pltpu.make_async_copy(source, store.at[s], store_sem.at[s])

    def load_sec(k, s):
        first, end = (
            0 if t < 0 else min(lines, (t + 1) * both - 2 * deep + 2 * LANES) for t in (s - 1, s)
        )
        length = end - first
        source = sec_hbm.at[k, pl.ds(first // 2, length // 2)].reshape(length, cols)
        return pltpu.make_async_copy(source, sec.at[k, pl.ds(first, length)], sec_sem.at[k, s])

    for copy in smalls:
        copy.start()
    for s in range(tiles):
        if s < EARLY:
            load_store(s).start()
        for k in range(scenes):
            load_sec(k, s).start()
    for s in range(EARLY, tiles):
        load_store(s).start()

    barrier = pltpu.get_barrier_semaphore()
    for exists, device in sides:
        @pl.when(exists)
        def _():
            pl.semaphore_signal(barrier, inc=1, device_id=device, device_id_type=MESH)

    @pl.when(jnp.logical_not(has_left))
    def _():
        halo[:, 0] = jnp.zeros(halo.shape[:1] + halo.shape[2:], BF16)

    @pl.when(jnp.logical_not(has_right))
    def _():
        halo[:, 1] = jnp.zeros(halo.shape[:1] + halo.shape[2:], BF16)

    def remote(source, target, sent, got, device):
        return pltpu.make_async_remote_copy(
            src_ref=source,
            dst_ref=target,
            send_sem=sent,
            recv_sem=got,
            device_id=device,
            device_id_type=MESH,
        )

    def edge_copy(s, side):
        return remote(
            edge.at[s, side],
            halo.at[s, 1 - side],
            edge_sem.at[s, side],
            halo_sem.at[s, 1 - side],
            {"range": col - 1 if side == 0 else col + 1},
        )

    def candidate_copy(s):
        return remote(store.at[s], other.at[s], xs_sem.at[s], xr_sem.at[s], {"scene": sibling})

    def handoff_copy(s):
        source = cur.at[s, scenes - 1]
        return remote(source, comm.at[0, s], hs_sem.at[s], hr_sem.at[s], {"scene": sibling})

    def ref_message(s):
        return jnp.where(s < EARLY, s + tiles, s)

    def line_copy(m):
        target = comm.at[1 - core, m]
        return remote(y_send.at[m], target, ys_sem.at[m], yr_sem.at[m], {"scene": outer})

    def relay_copy(s):
        source = comm.at[core, ref_message(s)]
        return remote(source, relayed.at[s], ls_sem.at[s], lr_sem.at[s], {"scene": sibling})

    def result_copy(s):
        return remote(ret_s.at[s], ret_r.at[s], rs_sem.at[s], rr_sem.at[s], {"scene": outer})

    for k in range(scenes):
        sec[k, lines:, :] = jnp.zeros((sec.shape[1] - lines, cols), BF16)

    for copy in smalls[:3]:
        copy.wait()
    table[...] = tap_table(azk[...], 2)

    def by_look(parts):
        shape = (parts, LOOK_AZ, GROUP, parts * deep)
        source = parts * (LOOK_AZ * iota(shape, 2) + iota(shape, 1)) + iota(shape, 0)
        return flag(iota(shape, 3) == source).reshape(parts * deep, parts * deep)

    def azimuth(s):
        order = by_look(1)
        for k in range(scenes):
            here = pl.ds(pl.multiple_of(s * rows, rows), rows)
            found = looked_up(table[...], azi[k : k + 1, here], azo[k : k + 1, here]).astype(BF16)
            for j in range(blocks):
                part = matmul(order, found[j * deep : (j + 1) * deep])
                tap_rows, shift = part[:, :LANES], part[:, LANES:].astype(jnp.int32)
                shape = (LOOK_AZ, GROUP, LANES)
                row = (LOOK_AZ * iota(shape, 1) + iota(shape, 0)).reshape(deep, LANES)
                start = iota((deep, LANES), 1) - 2 * (row + shift + (margin - 3))
                for p in range(2):
                    for t in range(2):
                        az_mat[
                            k, j, p * deep : (p + 1) * deep, t * LANES : (t + 1) * LANES
                        ] = banded(tap_rows, start + (t * LANES - p), 2 * taps)
            for j in range(blocks):
                first = pl.multiple_of(s * both + j * 2 * deep, 2 * deep)
                found = matmul(az_mat[k, j], sec[k, pl.ds(first, 2 * LANES), :])
                z[s, k, j * 2 * deep : (j + 1) * 2 * deep, :] = found.astype(BF16)
            which = iota((2 * margin, cols), 0)
            which = jnp.where(which < margin, which, which + cols - 2 * margin)
            ends = matmul(flag(iota((2 * margin, cols), 1) == which), z[s, k], ((1,), (1,)))
            ends = ends.astype(BF16)
            edge[s, 0, k] = ends[:margin]
            edge[s, 1, k] = ends[margin:]

    def send_edges(s):
        @pl.when(has_left)
        def _():
            edge_copy(s, 0).start()

        @pl.when(has_right)
        def _():
            edge_copy(s, 1).start()

    def range_step(s):
        @pl.when(has_left)
        def _():
            edge_copy(s, 1).wait_recv()

        @pl.when(has_right)
        def _():
            edge_copy(s, 0).wait_recv()

        for k in range(scenes):
            beside = jnp.concatenate([halo[s, 0, k], halo[s, 1, k]], 0)
            total = matmul(z[s, k], rg_mat[k])
            total = total + matmul(beside, rg_halo[k], ((0,), (0,)))
            cur[s, k] = total.astype(BF16)

    def line_send(s, from_relay):
        owner_chip = lax.div(owner_ref[s], 2)
        value = cur[s, core * (scenes - 1)]
        if from_relay:
            beyond = (is_r & (owner_chip < chip)) | (is_l & (owner_chip > chip))
            value = jnp.where(beyond, relayed[s], value)
        m = ref_message(s)
        y_send[m] = jnp.where(owner_chip == chip, own[s], value)
        line_copy(m).start()

    def choose(s):
        candidate_copy(s).wait_recv()
        order = by_look(2)
        for j in range(blocks):
            at = slice(j * 2 * deep, (j + 1) * 2 * deep)
            chosen = jnp.where(owner_ref[s] == sibling, other[s, at, :], store[s, at, :])
            own[s, at, :] = matmul(order, chosen).astype(BF16)

    def hands_on(s):
        even = lax.rem(s, 2) == 0
        return (s < EARLY) & ((r_up & even) | (l_up & jnp.logical_not(even)))

    def gets_handed(s):
        even = lax.rem(s, 2) == 0
        return (s < EARLY) & ((l_up & even) | (r_up & jnp.logical_not(even)))

    lane = iota((cols, LANES), 1) & (GROUP - 1)
    start = LOOK_RG * lane
    place = iota((cols, LANES), 0)
    mean = flag((place >= start) & (place < start + LOOK_RG))
    lane_group = iota((looks, LANES), 1)

    def multilooked(count, terms):
        sums = [[] for _ in range(count)]
        for j in range(blocks):
            total = None
            for l in range(LOOK_AZ):
                new = terms(j, l)
                total = new if total is None else [a + b for a, b in zip(total, new)]
            for one, value in zip(sums, total):
                one.append(value)
        stacked = jnp.concatenate([value for one in sums for value in one], 0)
        high = stacked.astype(BF16)
        low = (stacked - high.astype(F32)).astype(BF16)
        found = (matmul(high, mean) + matmul(low, mean)) * (1.0 / (LOOK_AZ * LOOK_RG))
        return [found[i * looks : (i + 1) * looks] for i in range(count)]

    def parts(read, j, l):
        first = j * 2 * deep + l * GROUP
        return [read(slice(first + p * deep, first + p * deep + GROUP)).astype(F32) for p in range(2)]

    def pack(values):
        out = values[-1]
        for i in range(len(values) - 2, -1, -1):
            out = jnp.where(lane_group < (i + 1) * GROUP, values[i], out)
        return out

    def own_terms(s):
        def terms(j, l):
            images = [parts(lambda at, k=k: cur[s, k, at, :], j, l) for k in range(scenes)]
            out = [power(image) for image in images]
            for one, two in zip(images[:-1], images[1:]):
                out += cross(one, two)
            return out

        found = multilooked(scenes + 2 * (scenes - 1), terms)
        for i, value in enumerate(found):
            stats[s, i] = value

    pl.semaphore_wait(barrier, sum(exists.astype(jnp.int32) for exists, _ in sides))
    for s in range(EARLY):
        load_store(s).wait()
        candidate_copy(s).start()
    for k in range(scenes):
        load_sec(k, 0).wait()
    azimuth(0)
    send_edges(0)
    smalls[-1].wait()
    for s in range(EARLY):
        choose(s)

        @pl.when(has_outer & jnp.logical_not(inner))
        def _():
            y_send[tiles + s] = own[s]
            line_copy(tiles + s).start()

    for s in range(EARLY, tiles):
        load_store(s).wait()
        candidate_copy(s).start()

    for copy in smalls[3:-1]:
        copy.wait()
    rg_table = tap_table(rgk[...], 1)
    for k in range(scenes):
        found = looked_up(rg_table, rgi[k : k + 1, :], rgo[k : k + 1, :])
        tap_rows, shift = found[:, :LANES], found[:, LANES:].astype(jnp.int32)
        lane = iota((cols, LANES), 1)
        start = iota((cols, LANES), 0) + shift + (margin - 3)
        for t in range(cols // LANES):
            found = banded(tap_rows, lane + (t * LANES + margin) - start, taps).astype(F32)
            rg_mat[k, t * LANES : (t + 1) * LANES, :] = jnp.transpose(found).astype(BF16)
        beside = jnp.where(lane < margin, lane, lane + cols)
        beside = jnp.where(lane < 2 * margin, beside, 4 * cols)
        outside = banded(tap_rows, beside - start, taps).astype(F32)
        rg_halo[k] = jnp.transpose(outside)[: 2 * margin].astype(BF16)

    def resample(s, more):
        if more:
            azimuth(s + 1)
            send_edges(s + 1)
        range_step(s)

        @pl.when(hands_on(s))
        def _():
            y_send[s] = cur[s, core * (scenes - 1)]
            line_copy(s).start()

        @pl.when(s >= EARLY)
        def _():
            choose(s)

            @pl.when(has_outer & jnp.logical_not(inner))
            def _():
                line_send(s, False)

        @pl.when(is_l)
        def _():
            handoff_copy(s).start()

        own_terms(s)

    def resample_step(s, carry):
        resample(s, True)
        return carry

    for s in range(1, tiles):
        for k in range(scenes):
            load_sec(k, s).wait()
    lax.fori_loop(0, tiles - 1, resample_step, 0)
    resample(tiles - 1, False)

    def compare(s, carry):
        def arrived():
            line_copy(ref_message(s)).wait_recv()
            relay_copy(s).start()

        def handed():
            relay_copy(s).wait_recv()

            @pl.when(inner)
            def _():
                line_send(s, True)

        pl.when(l_up)(arrived)
        pl.when(is_r & has_prev)(handed)
        pl.when(r_up)(arrived)
        pl.when(is_l & has_next)(handed)

        @pl.when(gets_handed(s))
        def _():
            line_copy(s).wait_recv()

        @pl.when(is_r)
        def _():
            handoff_copy(s).wait_recv()

        @pl.when(r_up)
        def _():
            def terms(j, l):
                last = parts(lambda at: cur[s, scenes - 1, at, :], j, l)
                after = parts(lambda at: comm[1, s, at, :], j, l)
                return cross(last, after) + [power(after)]

            re, im, strength = multilooked(3, terms)
            coherent = coherence(re, im, stats[s, scenes - 1], strength)
            ret_s[s] = pack([re, im, re, im, coherent])
            result_copy(s).start()

        owner_chip = lax.div(owner_ref[s], 2)
        direct = (is_l & (owner_chip < chip)) | (is_r & (owner_chip > chip))
        far = jnp.where(direct, comm[core, ref_message(s)], relayed[s])
        ref[...] = jnp.where(owner_chip == chip, own[s], far)

        @pl.when(me == 0)
        def _():
            comm[0, s] = ref[...]

        def terms(j, l):
            images = [parts(lambda at, k=k: cur[s, k, at, :], j, l) for k in range(scenes)]
            given = parts(lambda at: ref[at, :], j, l)
            before = parts(lambda at: comm[0, s, at, :], j, l)
            out = cross(before, images[0]) + [power(before)]
            for image in images:
                out += cross(given, image)
            return out

        found = multilooked(3 + 2 * scenes, terms)
        strength = found[2]
        for k in range(scenes):
            if k == 0:
                re, im = found[0], found[1]
            else:
                re, im = stats[s, scenes + 2 * (k - 1)], stats[s, scenes + 2 * (k - 1) + 1]
            coherent = coherence(re, im, strength, stats[s, k])
            strength = stats[s, k]
            packed[k, s] = pack([found[3 + 2 * k], found[4 + 2 * k], re, im, coherent])
        return carry

    lax.fori_loop(0, tiles, compare, 0)

    def settle(s, carry):
        @pl.when(l_up)
        def _():
            result_copy(s).wait_recv()
            owner_chip = lax.div(owner_ref[s], 2)
            back = ((s < EARLY) & (lax.rem(s, 2) == 1)) | ((s >= EARLY) & (owner_chip < chip))
            returned = back & (lane_group >= 2 * GROUP)
            packed[0, s] = jnp.where(returned, ret_r[s], packed[0, s])

        return carry

    lax.fori_loop(0, tiles, settle, 0)
    for k in range(scenes):
        planes = jnp.transpose(packed[k].reshape(tiles * looks, LANES))
        planes = [planes[i * GROUP : (i + 1) * GROUP] for i in range(5)]
        pair_ref[k, 0], pair_ref[k, 1], seq_ref[k, 0], seq_ref[k, 1], coh_ref[k] = planes

    def finish(s, carry):
        candidate_copy(s).wait_send()

        @pl.when(is_l)
        def _():
            handoff_copy(s).wait_send()

        @pl.when(has_outer)
        def _():
            line_copy(ref_message(s)).wait_send()
            relay_copy(s).wait_send()

        @pl.when(hands_on(s))
        def _():
            line_copy(s).wait_send()

        @pl.when(r_up)
        def _():
            result_copy(s).wait_send()

        @pl.when(has_left)
        def _():
            edge_copy(s, 0).wait_send()

        @pl.when(has_right)
        def _():
            edge_copy(s, 1).wait_send()

        return carry

    lax.fori_loop(0, tiles, finish, 0)


def write_out(*refs):
    count = len(refs) // 2
    copies = [
        pltpu.make_async_copy(refs[i], refs[count + i], refs[-1].at[i]) for i in range(count)
    ]
    for copy in copies:
        copy.start()
    for copy in copies:
        copy.wait()


def local(n_scene, n_range, *operands):
    secondary, store, owner, az_kernel, rg_kernel = operands[:5]
    operands = operands[:3] + (az_kernel.T, rg_kernel.T) + operands[5:]
    operands = [pltpu.with_memory_space_constraint(value, pltpu.HBM) for value in operands]
    scenes, length, _, cols = secondary.shape
    _, tiles, rows = store.shape[:3]
    count, taps = az_kernel.shape
    margin = (length - tiles * rows) // 2
    looks, cells = rows // LOOK_AZ, cols // LOOK_RG
    deep = LOOK_AZ * GROUP
    both = 2 * rows
    image = (both, cols)
    strip = tiles * looks
    dma = pltpu.SemaphoreType.DMA
    vmem = pltpu.VMEM
    home = pl.BlockSpec(memory_space=vmem)
    hbm = pl.BlockSpec(memory_space=pltpu.HBM)
    dims = (scenes, tiles, rows, cols, margin, taps, n_scene, n_range)
    results = pl.pallas_call(
        functools.partial(kernel_body, dims),
        out_shape=(
            jax.ShapeDtypeStruct((scenes, 2, cells, strip), F32),
            jax.ShapeDtypeStruct((scenes, 2, cells, strip), F32),
            jax.ShapeDtypeStruct((scenes, cells, strip), F32),
        ),
        in_specs=[hbm] * len(operands),
        out_specs=(home, home, home),
        scratch_shapes=[
            pltpu.SMEM(owner.shape, jnp.int32),
            vmem((taps, count), F32),
            vmem((taps, count), F32),
            vmem((scenes, tiles * rows), jnp.int32),
            vmem((scenes, tiles * rows), jnp.int32),
            vmem((scenes, cols), jnp.int32),
            vmem((scenes, cols), jnp.int32),
            vmem((scenes, 2 * (tiles * rows - deep + LANES), cols), BF16),
            vmem((tiles,) + image, BF16),
            vmem((tiles,) + image, BF16),
            vmem((tiles,) + image, BF16),
            vmem((tiles, scenes) + image, BF16),
            vmem((tiles, scenes) + image, BF16),
            vmem((scenes, rows // deep, 2 * deep, 2 * LANES), BF16),
            vmem((scenes, cols, cols), BF16),
            vmem((scenes, 2 * margin, cols), BF16),
            vmem((count + GROUP, 2 * LANES), BF16),
            vmem((tiles, 2, scenes, margin, both), BF16),
            vmem((tiles, 2, scenes, margin, both), BF16),
            vmem((2, tiles + EARLY) + image, BF16),
            vmem((tiles,) + image, BF16),
            vmem((tiles + EARLY,) + image, BF16),
            vmem(image, BF16),
            vmem((tiles, scenes + 2 * (scenes - 1), looks, LANES), F32),
            vmem((scenes, tiles, looks, LANES), F32),
            vmem((tiles, looks, LANES), F32),
            vmem((tiles, looks, LANES), F32),
            dma((7,)),
            dma((scenes, tiles)),
            dma((tiles,)),
            dma((tiles, 2)),
            dma((tiles, 2)),
        ]
        + [dma((tiles,))] * 4
        + [dma((tiles + EARLY,))] * 2
        + [dma((tiles,))] * 4,
        compiler_params=pltpu.CompilerParams(
            collective_id=0, has_side_effects=True, vmem_limit_bytes=VMEM_BYTES
        ),
    )(*operands)
    results = pl.pallas_call(
        write_out,
        out_shape=[jax.ShapeDtypeStruct(value.shape, F32) for value in results],
        in_specs=[hbm] * len(results),
        out_specs=[hbm] * len(results),
        scratch_shapes=[dma((len(results),))],
    )(*[pltpu.with_memory_space_constraint(value, pltpu.HBM) for value in results])
    return tuple(jnp.swapaxes(value, -1, -2) for value in results)


def solution(mesh):
    in_specs = (
        P(("parts", "scene"), None, None, "range"),
        P(("parts", "scene"), None, None, None, "range"),
        P("parts"),
        P(),
        P(),
        P(("parts", "scene"), None),
        P(("parts", "scene"), None),
        P(("parts", "scene"), "range"),
        P(("parts", "scene"), "range"),
    )
    out_specs = (
        P(("parts", "scene"), None, None, "range"),
        P(("parts", "scene"), None, None, "range"),
        P(("parts", "scene"), None, "range"),
    )
    body = functools.partial(local, mesh.shape["scene"], mesh.shape["range"])
    return jax.shard_map(body, mesh=mesh, in_specs=in_specs, out_specs=out_specs, check_vma=False)
```

```python
import functools

import jax
import jax.numpy as jnp
from jax import lax
from jax.experimental import pallas as pl
from jax.experimental.pallas import tpu as pltpu
from jax.sharding import PartitionSpec as P

LOOK_AZ = 4
LOOK_RG = 16
LANES = 128
GROUP = 16
EARLY = 2
VMEM_BYTES = 32 << 20

eps_power = 1e-06
F32 = jnp.float32
BF16 = jnp.bfloat16
MESH = pl.DeviceIdType.MESH


def iota(shape, dim):
    return lax.broadcasted_iota(jnp.int32, shape, dim)


def flag(condition):
    return jnp.where(condition, 1.0, 0.0).astype(BF16)


def matmul(a, b, contract=((1,), (0,))):
    return lax.dot_general(a, b, (contract, ((), ())), preferred_element_type=F32)


def tap_table(kernel, stride):
    taps, count = kernel.shape
    place = flag(iota((taps, LANES), 1) == stride * iota((taps, LANES), 0))
    spread = matmul(kernel.astype(BF16), place, ((0,), (0,))).astype(BF16)
    ones = flag(iota((GROUP, LANES), 0) == 0)
    return jnp.concatenate(
        [
            jnp.concatenate([spread, jnp.zeros((count, LANES), BF16)], 1),
            jnp.concatenate([jnp.zeros((GROUP, LANES), BF16), ones], 1),
        ],
        0,
    )


def looked_up(table, index, offset):
    count = table.shape[0] - GROUP
    length = index.shape[1]
    one_hot = flag(iota((count, length), 0) == index)
    shift = jnp.broadcast_to(offset.astype(F32), (GROUP, length)).astype(BF16)
    return matmul(jnp.concatenate([one_hot, shift], 0), table, ((0,), (0,)))


def banded(taps, place, reach):
    if reach & (reach - 1):
        inside = (place >= 0) & (place < reach)
    else:
        inside = (place & -reach) == 0
    picked = jnp.take_along_axis(taps, place & (LANES - 1), axis=1, mode="promise_in_bounds")
    return jnp.where(inside, picked, 0.0).astype(BF16)


def cross(a, b):
    return [a[0] * b[0] + a[1] * b[1], a[1] * b[0] - a[0] * b[1]]


def power(a):
    return a[0] * a[0] + a[1] * a[1]


def coherence(re, im, first, second):
    return jnp.sqrt(re * re + im * im) / jnp.sqrt(first * second + eps_power)


def kernel_body(
    dims,
    sec_hbm, store_hbm, owner_hbm, azk_hbm, rgk_hbm, azo_hbm, azi_hbm, rgo_hbm, rgi_hbm,
    pair_ref, seq_ref, coh_ref,
    owner_ref, azk, rgk, azo, azi, rgo, rgi,
    sec, store, other, own, z, cur, az_mat, rg_mat, rg_halo, table, edge, halo,
    comm, relayed, y_send, ref, stats, packed, ret_s, ret_r,
    small_sem, sec_sem, store_sem, edge_sem, halo_sem, xs_sem, xr_sem, hs_sem, hr_sem,
    ys_sem, yr_sem, ls_sem, lr_sem, rs_sem, rr_sem,
):
    scenes, tiles, rows, cols, margin, taps, n_scene, n_range = dims
    looks = rows // LOOK_AZ
    both = 2 * rows
    deep = LOOK_AZ * GROUP
    blocks = rows // deep
    lines = 2 * (tiles * rows + 2 * margin)
    me = lax.axis_index("scene")
    col = lax.axis_index("range")
    core, chip = lax.rem(me, 2), lax.div(me, 2)
    is_l, is_r = core == 0, core == 1
    sibling = me + 1 - 2 * core
    outer = me - 1 + 2 * core
    has_prev, has_next = chip > 0, chip < n_scene // 2 - 1
    inner = has_prev & has_next
    l_up, r_up = is_l & has_prev, is_r & has_next
    has_outer = l_up | r_up
    has_left, has_right = col > 0, col < n_range - 1
    always = me >= 0
    sides = (
        (has_left, {"range": col - 1}),
        (has_right, {"range": col + 1}),
        (always, {"scene": sibling}),
        (has_outer, {"scene": outer}),
    )

    smalls = [
        pltpu.make_async_copy(source, target, small_sem.at[i])
        for i, (source, target) in enumerate(
            (
                (azk_hbm, azk), (azo_hbm, azo), (azi_hbm, azi), (rgk_hbm, rgk),
                (rgo_hbm, rgo), (rgi_hbm, rgi), (owner_hbm, owner_ref),
            )
        )
    ]

    def load_store(s):
        source = store_hbm.reshape(tiles, both, cols).at[s]
        return pltpu.make_async_copy(source, store.at[s], store_sem.at[s])

    def load_sec(k, s):
        first, end = (
            0 if t < 0 else min(lines, (t + 1) * both - 2 * deep + 2 * LANES) for t in (s - 1, s)
        )
        length = end - first
        source = sec_hbm.at[k, pl.ds(first // 2, length // 2)].reshape(length, cols)
        return pltpu.make_async_copy(source, sec.at[k, pl.ds(first, length)], sec_sem.at[k, s])

    for copy in smalls:
        copy.start()
    for s in range(tiles):
        if s < EARLY:
            load_store(s).start()
        for k in range(scenes):
            load_sec(k, s).start()
    for s in range(EARLY, tiles):
        load_store(s).start()

    barrier = pltpu.get_barrier_semaphore()
    for exists, device in sides:
        @pl.when(exists)
        def _():
            pl.semaphore_signal(barrier, inc=1, device_id=device, device_id_type=MESH)

    @pl.when(jnp.logical_not(has_left))
    def _():
        halo[:, 0] = jnp.zeros(halo.shape[:1] + halo.shape[2:], BF16)

    @pl.when(jnp.logical_not(has_right))
    def _():
        halo[:, 1] = jnp.zeros(halo.shape[:1] + halo.shape[2:], BF16)

    def remote(source, target, sent, got, device):
        return pltpu.make_async_remote_copy(
            src_ref=source,
            dst_ref=target,
            send_sem=sent,
            recv_sem=got,
            device_id=device,
            device_id_type=MESH,
        )

    def edge_copy(s, side):
        return remote(
            edge.at[s, side],
            halo.at[s, 1 - side],
            edge_sem.at[s, side],
            halo_sem.at[s, 1 - side],
            {"range": col - 1 if side == 0 else col + 1},
        )

    def candidate_copy(s):
        return remote(store.at[s], other.at[s], xs_sem.at[s], xr_sem.at[s], {"scene": sibling})

    def handoff_copy(s):
        source = cur.at[s, scenes - 1]
        return remote(source, comm.at[0, s], hs_sem.at[s], hr_sem.at[s], {"scene": sibling})

    def ref_message(s):
        return jnp.where(s < EARLY, s + tiles, s)

    def line_copy(m):
        target = comm.at[1 - core, m]
        return remote(y_send.at[m], target, ys_sem.at[m], yr_sem.at[m], {"scene": outer})

    def relay_copy(s):
        source = comm.at[core, ref_message(s)]
        return remote(source, relayed.at[s], ls_sem.at[s], lr_sem.at[s], {"scene": sibling})

    def result_copy(s):
        return remote(ret_s.at[s], ret_r.at[s], rs_sem.at[s], rr_sem.at[s], {"scene": outer})

    for k in range(scenes):
        sec[k, lines:, :] = jnp.zeros((sec.shape[1] - lines, cols), BF16)

    for copy in smalls[:3]:
        copy.wait()
    table[...] = tap_table(azk[...], 2)

    def by_look(parts):
        shape = (parts, LOOK_AZ, GROUP, parts * deep)
        source = parts * (LOOK_AZ * iota(shape, 2) + iota(shape, 1)) + iota(shape, 0)
        return flag(iota(shape, 3) == source).reshape(parts * deep, parts * deep)

    def azimuth(s):
        order = by_look(1)
        for k in range(scenes):
            here = pl.ds(pl.multiple_of(s * rows, rows), rows)
            found = looked_up(table[...], azi[k : k + 1, here], azo[k : k + 1, here]).astype(BF16)
            for j in range(blocks):
                part = matmul(order, found[j * deep : (j + 1) * deep])
                tap_rows, shift = part[:, :LANES], part[:, LANES:].astype(jnp.int32)
                shape = (LOOK_AZ, GROUP, LANES)
                row = (LOOK_AZ * iota(shape, 1) + iota(shape, 0)).reshape(deep, LANES)
                start = iota((deep, LANES), 1) - 2 * (row + shift + (margin - 3))
                for p in range(2):
                    for t in range(2):
                        az_mat[
                            k, j, p * deep : (p + 1) * deep, t * LANES : (t + 1) * LANES
                        ] = banded(tap_rows, start + (t * LANES - p), 2 * taps)
            for j in range(blocks):
                first = pl.multiple_of(s * both + j * 2 * deep, 2 * deep)
                found = matmul(az_mat[k, j], sec[k, pl.ds(first, 2 * LANES), :])
                z[s, k, j * 2 * deep : (j + 1) * 2 * deep, :] = found.astype(BF16)
            which = iota((2 * margin, cols), 0)
            which = jnp.where(which < margin, which, which + cols - 2 * margin)
            ends = matmul(flag(iota((2 * margin, cols), 1) == which), z[s, k], ((1,), (1,)))
            ends = ends.astype(BF16)
            edge[s, 0, k] = ends[:margin]
            edge[s, 1, k] = ends[margin:]

    def send_edges(s):
        @pl.when(has_left)
        def _():
            edge_copy(s, 0).start()

        @pl.when(has_right)
        def _():
            edge_copy(s, 1).start()

    def range_step(s):
        @pl.when(has_left)
        def _():
            edge_copy(s, 1).wait_recv()

        @pl.when(has_right)
        def _():
            edge_copy(s, 0).wait_recv()

        for k in range(scenes):
            beside = jnp.concatenate([halo[s, 0, k], halo[s, 1, k]], 0)
            total = matmul(z[s, k], rg_mat[k])
            total = total + matmul(beside, rg_halo[k], ((0,), (0,)))
            cur[s, k] = total.astype(BF16)

    def line_send(s, from_relay):
        owner_chip = lax.div(owner_ref[s], 2)
        value = cur[s, core * (scenes - 1)]
        if from_relay:
            beyond = (is_r & (owner_chip < chip)) | (is_l & (owner_chip > chip))
            value = jnp.where(beyond, relayed[s], value)
        m = ref_message(s)
        y_send[m] = jnp.where(owner_chip == chip, own[s], value)
        line_copy(m).start()

    def choose(s):
        candidate_copy(s).wait_recv()
        order = by_look(2)
        for j in range(blocks):
            at = slice(j * 2 * deep, (j + 1) * 2 * deep)
            chosen = jnp.where(owner_ref[s] == sibling, other[s, at, :], store[s, at, :])
            own[s, at, :] = matmul(order, chosen).astype(BF16)

    def hands_on(s):
        even = lax.rem(s, 2) == 0
        return (s < EARLY) & ((r_up & even) | (l_up & jnp.logical_not(even)))

    def gets_handed(s):
        even = lax.rem(s, 2) == 0
        return (s < EARLY) & ((l_up & even) | (r_up & jnp.logical_not(even)))

    lane = iota((cols, LANES), 1) & (GROUP - 1)
    start = LOOK_RG * lane
    place = iota((cols, LANES), 0)
    mean = flag((place >= start) & (place < start + LOOK_RG))
    lane_group = iota((looks, LANES), 1)

    def multilooked(count, terms):
        sums = [[] for _ in range(count)]
        for j in range(blocks):
            total = None
            for l in range(LOOK_AZ):
                new = terms(j, l)
                total = new if total is None else [a + b for a, b in zip(total, new)]
            for one, value in zip(sums, total):
                one.append(value)
        stacked = jnp.concatenate([value for one in sums for value in one], 0)
        high = stacked.astype(BF16)
        low = (stacked - high.astype(F32)).astype(BF16)
        found = (matmul(high, mean) + matmul(low, mean)) * (1.0 / (LOOK_AZ * LOOK_RG))
        return [found[i * looks : (i + 1) * looks] for i in range(count)]

    def parts(read, j, l):
        first = j * 2 * deep + l * GROUP
        return [read(slice(first + p * deep, first + p * deep + GROUP)).astype(F32) for p in range(2)]

    def pack(values):
        out = values[-1]
        for i in range(len(values) - 2, -1, -1):
            out = jnp.where(lane_group < (i + 1) * GROUP, values[i], out)
        return out

    def own_terms(s):
        def terms(j, l):
            images = [parts(lambda at, k=k: cur[s, k, at, :], j, l) for k in range(scenes)]
            out = [power(image) for image in images]
            for one, two in zip(images[:-1], images[1:]):
                out += cross(one, two)
            return out

        found = multilooked(scenes + 2 * (scenes - 1), terms)
        for i, value in enumerate(found):
            stats[s, i] = value

    pl.semaphore_wait(barrier, sum(exists.astype(jnp.int32) for exists, _ in sides))
    for s in range(EARLY):
        load_store(s).wait()
        candidate_copy(s).start()
    for k in range(scenes):
        load_sec(k, 0).wait()
    azimuth(0)
    send_edges(0)
    smalls[-1].wait()
    for s in range(EARLY):
        choose(s)

        @pl.when(has_outer & jnp.logical_not(inner))
        def _():
            y_send[tiles + s] = own[s]
            line_copy(tiles + s).start()

    for s in range(EARLY, tiles):
        load_store(s).wait()
        candidate_copy(s).start()

    for copy in smalls[3:-1]:
        copy.wait()
    rg_table = tap_table(rgk[...], 1)
    for k in range(scenes):
        found = looked_up(rg_table, rgi[k : k + 1, :], rgo[k : k + 1, :])
        tap_rows, shift = found[:, :LANES], found[:, LANES:].astype(jnp.int32)
        lane = iota((cols, LANES), 1)
        start = iota((cols, LANES), 0) + shift + (margin - 3)
        for t in range(cols // LANES):
            found = banded(tap_rows, lane + (t * LANES + margin) - start, taps).astype(F32)
            rg_mat[k, t * LANES : (t + 1) * LANES, :] = jnp.transpose(found).astype(BF16)
        beside = jnp.where(lane < margin, lane, lane + cols)
        beside = jnp.where(lane < 2 * margin, beside, 4 * cols)
        outside = banded(tap_rows, beside - start, taps).astype(F32)
        rg_halo[k] = jnp.transpose(outside)[: 2 * margin].astype(BF16)

    def resample(s, more):
        if more:
            azimuth(s + 1)
            send_edges(s + 1)
        range_step(s)

        @pl.when(hands_on(s))
        def _():
            y_send[s] = cur[s, core * (scenes - 1)]
            line_copy(s).start()

        @pl.when(s >= EARLY)
        def _():
            choose(s)

            @pl.when(has_outer & jnp.logical_not(inner))
            def _():
                line_send(s, False)

        @pl.when(is_l)
        def _():
            handoff_copy(s).start()

        own_terms(s)

    def resample_step(s, carry):
        resample(s, True)
        return carry

    for s in range(1, tiles):
        for k in range(scenes):
            load_sec(k, s).wait()
    lax.fori_loop(0, tiles - 1, resample_step, 0)
    resample(tiles - 1, False)

    def compare(s, carry):
        def arrived():
            line_copy(ref_message(s)).wait_recv()
            relay_copy(s).start()

        def handed():
            relay_copy(s).wait_recv()

            @pl.when(inner)
            def _():
                line_send(s, True)

        pl.when(l_up)(arrived)
        pl.when(is_r & has_prev)(handed)
        pl.when(r_up)(arrived)
        pl.when(is_l & has_next)(handed)

        @pl.when(gets_handed(s))
        def _():
            line_copy(s).wait_recv()

        @pl.when(is_r)
        def _():
            handoff_copy(s).wait_recv()

        @pl.when(r_up)
        def _():
            def terms(j, l):
                last = parts(lambda at: cur[s, scenes - 1, at, :], j, l)
                after = parts(lambda at: comm[1, s, at, :], j, l)
                return cross(last, after) + [power(after)]

            re, im, strength = multilooked(3, terms)
            coherent = coherence(re, im, stats[s, scenes - 1], strength)
            ret_s[s] = pack([re, im, re, im, coherent])
            result_copy(s).start()

        owner_chip = lax.div(owner_ref[s], 2)
        direct = (is_l & (owner_chip < chip)) | (is_r & (owner_chip > chip))
        far = jnp.where(direct, comm[core, ref_message(s)], relayed[s])
        ref[...] = jnp.where(owner_chip == chip, own[s], far)

        @pl.when(me == 0)
        def _():
            comm[0, s] = ref[...]

        def terms(j, l):
            images = [parts(lambda at, k=k: cur[s, k, at, :], j, l) for k in range(scenes)]
            given = parts(lambda at: ref[at, :], j, l)
            before = parts(lambda at: comm[0, s, at, :], j, l)
            out = cross(before, images[0]) + [power(before)]
            for image in images:
                out += cross(given, image)
            return out

        found = multilooked(3 + 2 * scenes, terms)
        strength = found[2]
        for k in range(scenes):
            if k == 0:
                re, im = found[0], found[1]
            else:
                re, im = stats[s, scenes + 2 * (k - 1)], stats[s, scenes + 2 * (k - 1) + 1]
            coherent = coherence(re, im, strength, stats[s, k])
            strength = stats[s, k]
            packed[k, s] = pack([found[3 + 2 * k], found[4 + 2 * k], re, im, coherent])
        return carry

    lax.fori_loop(0, tiles, compare, 0)

    def settle(s, carry):
        @pl.when(l_up)
        def _():
            result_copy(s).wait_recv()
            owner_chip = lax.div(owner_ref[s], 2)
            back = ((s < EARLY) & (lax.rem(s, 2) == 1)) | ((s >= EARLY) & (owner_chip < chip))
            returned = back & (lane_group >= 2 * GROUP)
            packed[0, s] = jnp.where(returned, ret_r[s], packed[0, s])

        return carry

    lax.fori_loop(0, tiles, settle, 0)
    for k in range(scenes):
        planes = jnp.transpose(packed[k].reshape(tiles * looks, LANES))
        planes = [planes[i * GROUP : (i + 1) * GROUP] for i in range(5)]
        pair_ref[k, 0], pair_ref[k, 1], seq_ref[k, 0], seq_ref[k, 1], coh_ref[k] = planes

    def finish(s, carry):
        candidate_copy(s).wait_send()

        @pl.when(is_l)
        def _():
            handoff_copy(s).wait_send()

        @pl.when(has_outer)
        def _():
            line_copy(ref_message(s)).wait_send()
            relay_copy(s).wait_send()

        @pl.when(hands_on(s))
        def _():
            line_copy(s).wait_send()

        @pl.when(r_up)
        def _():
            result_copy(s).wait_send()

        @pl.when(has_left)
        def _():
            edge_copy(s, 0).wait_send()

        @pl.when(has_right)
        def _():
            edge_copy(s, 1).wait_send()

        return carry

    lax.fori_loop(0, tiles, finish, 0)


def local(n_scene, n_range, *operands):
    secondary, store, owner, az_kernel, rg_kernel = operands[:5]
    operands = operands[:3] + (az_kernel.T, rg_kernel.T) + operands[5:]
    operands = [pltpu.with_memory_space_constraint(value, pltpu.HBM) for value in operands]
    scenes, length, _, cols = secondary.shape
    _, tiles, rows = store.shape[:3]
    count, taps = az_kernel.shape
    margin = (length - tiles * rows) // 2
    looks, cells = rows // LOOK_AZ, cols // LOOK_RG
    deep = LOOK_AZ * GROUP
    both = 2 * rows
    image = (both, cols)
    strip = tiles * looks
    dma = pltpu.SemaphoreType.DMA
    vmem = pltpu.VMEM
    home = pl.BlockSpec(memory_space=vmem)
    hbm = pl.BlockSpec(memory_space=pltpu.HBM)
    dims = (scenes, tiles, rows, cols, margin, taps, n_scene, n_range)
    results = pl.pallas_call(
        functools.partial(kernel_body, dims),
        out_shape=(
            jax.ShapeDtypeStruct((scenes, 2, cells, strip), F32),
            jax.ShapeDtypeStruct((scenes, 2, cells, strip), F32),
            jax.ShapeDtypeStruct((scenes, cells, strip), F32),
        ),
        in_specs=[hbm] * len(operands),
        out_specs=(home, home, home),
        scratch_shapes=[
            pltpu.SMEM(owner.shape, jnp.int32),
            vmem((taps, count), F32),
            vmem((taps, count), F32),
            vmem((scenes, tiles * rows), jnp.int32),
            vmem((scenes, tiles * rows), jnp.int32),
            vmem((scenes, cols), jnp.int32),
            vmem((scenes, cols), jnp.int32),
            vmem((scenes, 2 * (tiles * rows - deep + LANES), cols), BF16),
            vmem((tiles,) + image, BF16),
            vmem((tiles,) + image, BF16),
            vmem((tiles,) + image, BF16),
            vmem((tiles, scenes) + image, BF16),
            vmem((tiles, scenes) + image, BF16),
            vmem((scenes, rows // deep, 2 * deep, 2 * LANES), BF16),
            vmem((scenes, cols, cols), BF16),
            vmem((scenes, 2 * margin, cols), BF16),
            vmem((count + GROUP, 2 * LANES), BF16),
            vmem((tiles, 2, scenes, margin, both), BF16),
            vmem((tiles, 2, scenes, margin, both), BF16),
            vmem((2, tiles + EARLY) + image, BF16),
            vmem((tiles,) + image, BF16),
            vmem((tiles + EARLY,) + image, BF16),
            vmem(image, BF16),
            vmem((tiles, scenes + 2 * (scenes - 1), looks, LANES), F32),
            vmem((scenes, tiles, looks, LANES), F32),
            vmem((tiles, looks, LANES), F32),
            vmem((tiles, looks, LANES), F32),
            dma((7,)),
            dma((scenes, tiles)),
            dma((tiles,)),
            dma((tiles, 2)),
            dma((tiles, 2)),
        ]
        + [dma((tiles,))] * 4
        + [dma((tiles + EARLY,))] * 2
        + [dma((tiles,))] * 4,
        compiler_params=pltpu.CompilerParams(
            collective_id=0, has_side_effects=True, vmem_limit_bytes=VMEM_BYTES
        ),
    )(*operands)
    return tuple(jnp.swapaxes(value, -1, -2) for value in results)


def solution(mesh):
    in_specs = (
        P(("parts", "scene"), None, None, "range"),
        P(("parts", "scene"), None, None, None, "range"),
        P("parts"),
        P(),
        P(),
        P(("parts", "scene"), None),
        P(("parts", "scene"), None),
        P(("parts", "scene"), "range"),
        P(("parts", "scene"), "range"),
    )
    out_specs = (
        P(("parts", "scene"), None, None, "range"),
        P(("parts", "scene"), None, None, "range"),
        P(("parts", "scene"), None, "range"),
    )
    body = functools.partial(local, mesh.shape["scene"], mesh.shape["range"])
    return jax.shard_map(body, mesh=mesh, in_specs=in_specs, out_specs=out_specs, check_vma=False)
```
